128 devices in a mesh: space: 16 (over z, y_lo, core), tracer: 8 (over x, y_hi).
Axes of the slice: x: 4, y: 4 (y_hi: 2, y_lo: 2; y = y_hi * 2 + y_lo), z: 4, core: 2. Of those that a mesh axis runs over, the one named last changes fastest.
Arguments:
- mixing_ratio_field: float32 [256, 2, 256, 256], P('tracer', None, 'space'), may hold values from 0.1 to 10
- eastward_face_cfl: float32 [2, 256, 256], P(None, 'space'), may hold values from 0.05 to 0.45
- northward_face_cfl: float32 [2, 256, 256], P(None, 'space'), may hold values from 0.05 to 0.45
- upward_face_cfl: float32 [2, 256, 256], P(None, 'space'), may hold values from 0.05 to 0.45
- thermal_anomaly: float32 [2, 256, 256], P(None, ('space', 'tracer')), may hold values from 0.8 to 1.2
- radiant_flux: float32 [2, 256, 256], P(None, ('space', 'tracer')), may hold values from 0.2 to 1
- daylight_mask: int32 [2, 256, 2], P(None, ('space', 'tracer')), may hold values from 0 to 1, as said below
- baseline_kinetic_coefficient: float32 [768], replicated, may hold values from 0.02 to 1
- arrhenius_barrier: float32 [768], replicated, may hold values from 0.5 to 3
- photodissociation_factor: float32 [768], replicated, may hold values from 0.02 to 1
- stoichiometry_table: int32 [3, 768], replicated, may hold values from 0 to 255
Outputs:
- result: float32 [256, 2, 256, 256], P(None, None, ('space', 'tracer'))
The draws below stay inside these ranges and needn't reach their ends.
Inputs may be any that keep to these rules, and one draw needn't show every extreme that they name: For every level l, row x below 128 and block b, daylight_mask[l, x, b] + daylight_mask[l, x + 128, b] == 1: a block and the block 128 rows further along the first dimension are never both sunlit or both dark.
All inputs are finite; a program needn't handle non-finite values.
Results may differ from the reference program's by a relative error of at most 0.0003.
Values sent between devices are 32-bit elements; how exact they have to be, the bound alone decides.
A program may use at most 64 MiB of HBM per device.

```python
import math
import jax
import jax.numpy as jnp
from jax import lax

S = 256
R = 768
PATCH_SIZE = 128
SECTIONS = 3
DAY_STEPS = 2
NIGHT_STEPS = 1
GRID_WIDTH_NORTH = 256
ALTITUDE_TIERS = 2
GRID_WIDTH_EAST = 256


def draw_daylight_mask(key, part):
    half_rows = GRID_WIDTH_EAST // 2
    scores = jax.random.randint(key, (ALTITUDE_TIERS, half_rows, GRID_WIDTH_NORTH // PATCH_SIZE), 0, half_rows)
    rows = lax.broadcasted_iota(jnp.int32, (ALTITUDE_TIERS, half_rows, GRID_WIDTH_NORTH // PATCH_SIZE), 1)
    first_half = (scores <= rows).astype(jnp.int32)
    return jnp.concatenate([first_half, 1 - first_half], axis=1)


def touch_ends(array, own_key, least, high):
    shape = array.shape
    index_at = [jax.random.randint(jax.random.fold_in(own_key, axis), (), 0, shape[axis]) for axis in range(len(shape))]
    array = array.at[tuple(index_at)].set(least)
    longest = shape.index(max(shape))
    index_at[longest] = (index_at[longest] + 1) % shape[longest]
    return array.at[tuple(index_at)].set(high)


def block_levels(own_key, dims, pieces, least, top_value):
    gain, own = 1.0, jax.random.fold_in(own_key, 6)
    for position, shards_of in pieces:
        draws = jnp.exp(jax.random.uniform(jax.random.fold_in(own, position), (shards_of,), jnp.float32, least / len(pieces), top_value / len(pieces)))
        gain = gain * jnp.repeat(draws, dims[position] // shards_of).reshape([-1 if axis == position else 1 for axis in range(len(dims))])
    return gain


def setup_inputs(seed: int = 0) -> dict:
    key_list = jax.random.split(jax.random.key(seed), 12)
    mixing_ratio_field = jnp.clip(jnp.exp(math.log(10.0) - 4.6051702 * jax.random.uniform(key_list[0], (S, ALTITUDE_TIERS, GRID_WIDTH_EAST, GRID_WIDTH_NORTH), jnp.float32) ** block_levels(key_list[0], (S, ALTITUDE_TIERS, GRID_WIDTH_EAST, GRID_WIDTH_NORTH), ((0, 8), (2, 16)), -0.2, 0.2)), 0.1, 10.0)
    eastward_face_cfl = jnp.clip(0.05 + 0.39999999 * jax.random.uniform(key_list[1], (ALTITUDE_TIERS, GRID_WIDTH_EAST, GRID_WIDTH_NORTH), jnp.float32) ** block_levels(key_list[1], (ALTITUDE_TIERS, GRID_WIDTH_EAST, GRID_WIDTH_NORTH), ((1, 16),), -0.2, 0.2), 0.05, 0.45)
    northward_face_cfl = jnp.clip(0.05 + 0.39999999 * jax.random.uniform(key_list[2], (ALTITUDE_TIERS, GRID_WIDTH_EAST, GRID_WIDTH_NORTH), jnp.float32) ** block_levels(key_list[2], (ALTITUDE_TIERS, GRID_WIDTH_EAST, GRID_WIDTH_NORTH), ((1, 16),), -0.2, 0.2), 0.05, 0.45)
    upward_face_cfl = jnp.clip(0.05 + 0.39999999 * jax.random.uniform(key_list[3], (ALTITUDE_TIERS, GRID_WIDTH_EAST, GRID_WIDTH_NORTH), jnp.float32) ** block_levels(key_list[3], (ALTITUDE_TIERS, GRID_WIDTH_EAST, GRID_WIDTH_NORTH), ((1, 16),), -0.2, 0.2), 0.05, 0.45)
    thermal_anomaly = jnp.clip(0.8 + 0.40000004 * jax.random.uniform(key_list[4], (ALTITUDE_TIERS, GRID_WIDTH_EAST, GRID_WIDTH_NORTH), jnp.float32) ** block_levels(key_list[4], (ALTITUDE_TIERS, GRID_WIDTH_EAST, GRID_WIDTH_NORTH), ((1, 128),), -0.2, 0.2), 0.8, 1.2)
    radiant_flux = jnp.clip(0.2 + 0.8 * jax.random.uniform(key_list[5], (ALTITUDE_TIERS, GRID_WIDTH_EAST, GRID_WIDTH_NORTH), jnp.float32) ** block_levels(key_list[5], (ALTITUDE_TIERS, GRID_WIDTH_EAST, GRID_WIDTH_NORTH), ((1, 128),), -0.2, 0.2), 0.2, 1.0)
    daylight_mask = draw_daylight_mask(jax.random.fold_in(key_list[11], 71), 0)
    baseline_kinetic_coefficient = jnp.clip(jnp.exp(jax.random.uniform(key_list[7], (R,), jnp.float32, math.log(0.02), math.log(1.0))), 0.02, 1.0)
    arrhenius_barrier = jnp.clip(jax.random.uniform(key_list[8], (R,), jnp.float32, 0.5, 3.0), 0.5, 3.0)
    photodissociation_factor = jnp.clip(jnp.exp(jax.random.uniform(key_list[9], (R,), jnp.float32, math.log(0.02), math.log(1.0))), 0.02, 1.0)
    stoichiometry_table = touch_ends(jax.random.randint(key_list[10], (3, R), 0, S), jax.random.fold_in(key_list[10], 1), 0, S - 1).astype(jnp.int32)
    return {"mixing_ratio_field": mixing_ratio_field, "eastward_face_cfl": eastward_face_cfl, "northward_face_cfl": northward_face_cfl, "upward_face_cfl": upward_face_cfl, "thermal_anomaly": thermal_anomaly, "radiant_flux": radiant_flux, "daylight_mask": daylight_mask, "baseline_kinetic_coefficient": baseline_kinetic_coefficient, "arrhenius_barrier": arrhenius_barrier, "photodissociation_factor": photodissociation_factor, "stoichiometry_table": stoichiometry_table}


def minmod(left_slope, right_slope):
    return 0.5 * (jnp.sign(left_slope) + jnp.sign(right_slope)) * jnp.minimum(jnp.abs(left_slope), jnp.abs(right_slope))


def face_flux(far_cell, near_cell, past_cell, courant):
    return courant * (near_cell + 0.5 * (1.0 - courant) * minmod(near_cell - far_cell, past_cell - near_cell))


def sweep_rows(field, courant):
    inner = field.shape[2] - 4
    fluxes = face_flux(field[:, :, 0:inner + 1], field[:, :, 1:inner + 2], field[:, :, 2:inner + 3], courant[None, :, 2:inner + 3])
    return field[:, :, 2:inner + 2] - (fluxes[:, :, 1:] - fluxes[:, :, :-1])


def sweep_cols(field, courant):
    fluxes = face_flux(jnp.roll(field, 2, axis=3), jnp.roll(field, 1, axis=3), field, courant[None])
    return field - (jnp.roll(fluxes, -1, axis=3) - fluxes)


def sweep_levels(field, courant):
    zero_layer = jnp.zeros_like(field[:, :1])
    lower_cells = jnp.concatenate([zero_layer, field[:, :-1]], axis=1)
    upper_cells = jnp.concatenate([field[:, 1:], zero_layer], axis=1)
    fluxes = face_flux(lower_cells, field, upper_cells, courant[None])
    inflow = jnp.concatenate([zero_layer, fluxes[:, :-1]], axis=1)
    return field - (fluxes - inflow)


def react_ref(field, warmth, glow, baseline_kinetic_coefficient, arrhenius_barrier, photodissociation_factor, stoichiometry_table, substeps, lit):
    species = field.shape[0]
    rates = baseline_kinetic_coefficient[:, None] * jnp.exp(-arrhenius_barrier[:, None] * (warmth[None, :] - 1.0))
    if lit:
        rates = rates + photodissociation_factor[:, None] * glow[None, :]
    step_size = 1.0 / substeps
    for sub_num in range(substeps):
        first_conc = field[stoichiometry_table[0]]
        second_conc = field[stoichiometry_table[1]]
        speed = rates * first_conc * second_conc
        produced = jax.ops.segment_sum(speed, stoichiometry_table[2], num_segments=species)
        consumed = jax.ops.segment_sum(rates * second_conc, stoichiometry_table[0], num_segments=species)
        consumed = consumed + jax.ops.segment_sum(rates * first_conc, stoichiometry_table[1], num_segments=species)
        field = (field + step_size * produced) / (1.0 + step_size * consumed)
    return field


def reference(mixing_ratio_field, eastward_face_cfl, northward_face_cfl, upward_face_cfl, thermal_anomaly, radiant_flux, daylight_mask, baseline_kinetic_coefficient, arrhenius_barrier, photodissociation_factor, stoichiometry_table):
    field = mixing_ratio_field
    padded_courant = jnp.pad(eastward_face_cfl, ((0, 0), (2, 2), (0, 0)))
    for section_num in range(SECTIONS):
        padded = jnp.pad(field, ((0, 0), (0, 0), (2, 2), (0, 0)))
        field = sweep_rows(padded, padded_courant)
        field = sweep_cols(field, northward_face_cfl)
        field = sweep_levels(field, upward_face_cfl)
    species = field.shape[0]
    blocks = jnp.moveaxis(field.reshape(species, -1, PATCH_SIZE), 1, 0)
    warm_patches = thermal_anomaly.reshape(-1, PATCH_SIZE)
    glow_blocks = radiant_flux.reshape(-1, PATCH_SIZE)
    flags = daylight_mask.reshape(-1)

    def one_block(items):
        block, warmth, glow, flag = items
        bright = react_ref(block, warmth, glow, baseline_kinetic_coefficient, arrhenius_barrier, photodissociation_factor, stoichiometry_table, DAY_STEPS, True)
        dark = react_ref(block, warmth, glow, baseline_kinetic_coefficient, arrhenius_barrier, photodissociation_factor, stoichiometry_table, NIGHT_STEPS, False)
        return jnp.where(flag == 1, bright, dark)

    reacted = lax.map(one_block, (blocks, warm_patches, glow_blocks, flags))
    return jnp.moveaxis(reacted, 0, 1).reshape(field.shape)
```

```python
import functools

import jax
import jax.numpy as jnp
from jax import lax
from jax.experimental import pallas as pl
from jax.experimental.pallas import tpu as pltpu
from jax.sharding import PartitionSpec as P

MESH = pl.DeviceIdType.MESH
F32 = jnp.float32

SECTIONS = 3
DAY_STEPS = 2
LOW, HIGH = 2 * SECTIONS, SECTIONS
GROUP = 8


def minmod(a, b):
    return jnp.maximum(jnp.minimum(a, jnp.maximum(b, 0.0)), jnp.minimum(b, 0.0))


def transport_kernel(
    strips,
    groups,
    field,
    ux,
    uy,
    uz,
    warm,
    glow,
    base,
    barrier_coef,
    photo,
    cells_out,
    rates_out,
    raw,
    first,
    second,
    third,
    turned,
    packed,
    coef,
    plain,
    edge_up,
    edge_down,
    got_low,
    got_high,
    rates,
    load_sem,
    halo_send,
    halo_recv,
    edge_send,
    edge_recv,
    all_send,
    all_recv,
    own_sem,
    rate_sem,
):
    s = lax.axis_index("space")
    t = lax.axis_index("tracer")
    n_groups = first.shape[0]
    rows = 16
    species_here = n_groups * GROUP
    has_low = s > 0
    has_high = s < strips - 1
    low, high = s - 1, s + 1

    def load(g, blk):
        return pltpu.make_async_copy(
            field.at[pl.ds(g * GROUP, GROUP), :, :, pl.ds(blk * 128, 128)],
            raw.at[blk, pl.ds(g * GROUP, GROUP)],
            load_sem.at[g, blk],
        )

    for g in range(n_groups):
        for blk in range(2):
            load(g, blk).start()

    door = pltpu.get_barrier_semaphore()
    for i in range(1, groups):
        pl.semaphore_signal(
            door, inc=1, device_id=(s, lax.rem(t + i, groups)), device_id_type=MESH
        )

    @pl.when(has_low)
    def _():
        pl.semaphore_signal(door, inc=1, device_id=(low, t), device_id_type=MESH)

    @pl.when(has_high)
    def _():
        pl.semaphore_signal(door, inc=1, device_id=(high, t), device_id_type=MESH)

    for q, u in enumerate((ux, uy, uz)):
        for blk in range(2):
            for l in range(2):
                plain[q, l, blk] = u[l, :, blk * 128 : blk * 128 + 128]
                edge_up[q, blk, l * 4 : l * 4 + 4] = u[l, rows - 4 : rows, blk * 128 : blk * 128 + 128]
                edge_down[q, blk, l * 4 : l * 4 + 4] = u[l, 0:4, blk * 128 : blk * 128 + 128]

    flat = raw.reshape(2 * species_here * 2 * rows, 128)

    def turn(g, row):
        for l in range(2):
            for blk in range(2):
                start = blk * (species_here * 2 * rows) + g * (GROUP * 2 * rows) + l * rows + row
                first[g, row + LOW, l, blk] = flat[pl.ds(start, GROUP, stride=2 * rows), :]

    pl.semaphore_wait(door, groups - 1 + jnp.where(has_low, 1, 0) + jnp.where(has_high, 1, 0))

    def halo_up(g):
        return pltpu.make_async_remote_copy(
            src_ref=first.at[g, pl.ds(rows, LOW)],
            dst_ref=first.at[g, pl.ds(0, LOW)],
            send_sem=halo_send.at[0, g],
            recv_sem=halo_recv.at[0, g],
            device_id=(high, t),
            device_id_type=MESH,
        )

    def halo_down(g):
        return pltpu.make_async_remote_copy(
            src_ref=first.at[g, pl.ds(LOW, HIGH)],
            dst_ref=first.at[g, pl.ds(LOW + rows, HIGH)],
            send_sem=halo_send.at[1, g],
            recv_sem=halo_recv.at[1, g],
            device_id=(low, t),
            device_id_type=MESH,
        )

    def coef_up():
        return pltpu.make_async_remote_copy(
            src_ref=edge_up,
            dst_ref=got_low,
            send_sem=edge_send.at[0],
            recv_sem=edge_recv.at[0],
            device_id=(high, t),
            device_id_type=MESH,
        )

    def coef_down():
        return pltpu.make_async_remote_copy(
            src_ref=edge_down,
            dst_ref=got_high,
            send_sem=edge_send.at[1],
            recv_sem=edge_recv.at[1],
            device_id=(low, t),
            device_id_type=MESH,
        )

    @pl.when(has_high)
    def _():
        coef_up().start()

    @pl.when(has_low)
    def _():
        coef_down().start()

    def send_edges(g, carry):
        load(g, 0).wait()
        load(g, 1).wait()
        for row in range(rows - LOW, rows):
            turn(g, row)

        @pl.when(has_high)
        def _():
            halo_up(g).start()

        for row in range(HIGH):
            turn(g, row)

        @pl.when(has_low)
        def _():
            halo_down(g).start()

        return carry

    lax.fori_loop(0, n_groups, send_edges, 0)

    def turn_rest(g, carry):
        for row in range(HIGH, rows - LOW):
            turn(g, row)
        return carry

    lax.fori_loop(0, n_groups, turn_rest, 0)

    zero = jnp.zeros((GROUP, 128), F32)

    @pl.when(jnp.logical_not(has_low))
    def _():
        for g in range(n_groups):
            for row in range(LOW):
                for l in range(2):
                    for blk in range(2):
                        first[g, row, l, blk] = zero
        for q in range(3):
            for blk in range(2):
                got_low[q, blk] = zero

    @pl.when(jnp.logical_not(has_high))
    def _():
        for g in range(n_groups):
            for row in range(HIGH):
                for l in range(2):
                    for blk in range(2):
                        first[g, LOW + rows + row, l, blk] = zero
        for q in range(3):
            for blk in range(2):
                got_high[q, blk] = zero

    lane = lax.broadcasted_iota(jnp.int32, (GROUP, 128), 1)
    is_first = lane == 0
    is_last = lane == 127

    def from_left(x0, x1):
        r0, r1 = pltpu.roll(x0, 1, 1), pltpu.roll(x1, 1, 1)
        return jnp.where(is_first, r1, r0), jnp.where(is_first, r0, r1)

    def from_right(x0, x1):
        r0, r1 = pltpu.roll(x0, 127, 1), pltpu.roll(x1, 127, 1)
        return jnp.where(is_last, r1, r0), jnp.where(is_last, r0, r1)

    def spread(row, get):
        for l in range(2):
            for q in range(3):
                pair = [jnp.broadcast_to(get(q, l, blk), (GROUP, 128)) for blk in range(2)]
                if q == 1:
                    pair = from_right(*pair)
                for blk in range(2):
                    coef[2 * q, row, l, blk] = pair[blk]
                    coef[2 * q + 1, row, l, blk] = 0.5 * (1.0 - pair[blk])

    def spread_own(row, carry):
        spread(row + 4, lambda q, l, blk: plain[q, l, blk, pl.ds(row, 1), :])
        return carry

    lax.fori_loop(0, rows, spread_own, 0)

    @pl.when(has_low)
    def _():
        coef_up().wait_recv()

    @pl.when(has_high)
    def _():
        coef_down().wait_recv()

    for i in range(4):
        spread(i, lambda q, l, blk: got_low[q, blk, l * 4 + i : l * 4 + i + 1])
    for i in range(3):
        spread(rows + 4 + i, lambda q, l, blk: got_high[q, blk, l * 4 + i : l * 4 + i + 1])

    four = [(l, blk) for l in range(2) for blk in range(2)]

    def one_step(read, lo, count, write):
        state = []
        for l, blk in four:
            c0, c1, c2 = read(lo - 2, l, blk), read(lo - 1, l, blk), read(lo, l, blk)
            d1, d2 = c1 - c0, c2 - c1
            flux = coef[0, lo + 4, l, blk] * (c1 + coef[1, lo + 4, l, blk] * minmod(d1, d2))
            state += [c2, d2, flux]

        def body(i, state):
            row = i + lo
            after, swept = [], []
            for n, (l, blk) in enumerate(four):
                c, d, flux = state[3 * n : 3 * n + 3]
                c_next = read(row + 1, l, blk)
                d_next = c_next - c
                flux_next = coef[0, row + 5, l, blk] * (
                    c + coef[1, row + 5, l, blk] * minmod(d, d_next)
                )
                swept.append(c - (flux_next - flux))
                after += [c_next, d_next, flux_next]
            for l in range(2):
                c0, c1 = swept[2 * l], swept[2 * l + 1]
                m0, m1 = from_left(c0, c1)
                d0, d1 = c0 - m0, c1 - m1
                e0, e1 = from_right(d0, d1)
                g0 = coef[2, row + 4, l, 0] * (c0 + coef[3, row + 4, l, 0] * minmod(d0, e0))
                g1 = coef[2, row + 4, l, 1] * (c1 + coef[3, row + 4, l, 1] * minmod(d1, e1))
                h0, h1 = from_left(g0, g1)
                swept[2 * l] = c0 - (g0 - h0)
                swept[2 * l + 1] = c1 - (g1 - h1)
            for blk in range(2):
                c0, c1 = swept[blk], swept[2 + blk]
                rise = c1 - c0
                g0 = coef[4, row + 4, 0, blk] * (c0 + coef[5, row + 4, 0, blk] * minmod(c0, rise))
                g1 = coef[4, row + 4, 1, blk] * (c1 + coef[5, row + 4, 1, blk] * minmod(rise, -c1))
                write(row, 0, blk, c0 - g0)
                write(row, 1, blk, c1 - (g1 - g0))
            return tuple(after)

        lax.fori_loop(0, count, body, tuple(state))

    def all_copy(g, i):
        to = lax.rem(t + i, groups)
        return pltpu.make_async_remote_copy(
            src_ref=packed.at[g, to],
            dst_ref=cells_out.at[pl.ds(t * species_here + g * GROUP, GROUP)],
            send_sem=all_send.at[g, i - 1],
            recv_sem=all_recv.at[g, i - 1],
            device_id=(s, to),
            device_id_type=MESH,
        )

    def own_copy(g):
        return pltpu.make_async_copy(
            packed.at[g, t],
            cells_out.at[pl.ds(t * species_here + g * GROUP, GROUP)],
            own_sem.at[g],
        )

    turned_flat = turned.reshape(groups * 8 * GROUP, 128)
    order = [i for i in range(1, groups) if i % 2 == 1] + [i for i in range(1, groups) if i % 2 == 0]

    def sweep_group(g, carry):
        @pl.when(has_low)
        def _():
            halo_up(g).wait_recv()

        @pl.when(has_high)
        def _():
            halo_down(g).wait_recv()

        def put2(row, l, blk, v):
            second[row + 4, l, blk] = v

        def put3(row, l, blk, v):
            third[row + 2, l, blk] = v

        def put4(row, l, blk, v):
            turned[row // 2, l * 4 + blk * 2 + row % 2] = v

        one_step(lambda row, l, blk: first[g, row + LOW, l, blk], -4, rows + 6, put2)
        one_step(lambda row, l, blk: second[row + 4, l, blk], -2, rows + 3, put3)
        one_step(lambda row, l, blk: third[row + 2, l, blk], 0, rows, put4)

        def pack(to, carry):
            for k in range(GROUP):
                packed[g, to, k] = turned_flat[pl.ds(to * (8 * GROUP) + k, 8, stride=GROUP), :]
            return carry

        lax.fori_loop(0, groups, pack, 0)
        for i in order:
            all_copy(g, i).start()
        own_copy(g).start()
        return carry

    lax.fori_loop(0, n_groups, sweep_group, 0)

    cold = 1.0 - warm[...]
    light = glow[...]
    reactions = rates.shape[0]

    def rate(i, carry):
        for j in range(8):
            r = i * 8 + j
            rates[r] = base[r] * jnp.exp(barrier_coef[r] * cold) + photo[r] * light
        return carry

    lax.fori_loop(0, reactions // 8, rate, 0)
    rate_copy = pltpu.make_async_copy(rates, rates_out, rate_sem)
    rate_copy.start()

    @pl.when(has_high)
    def _():
        coef_up().wait_send()

    @pl.when(has_low)
    def _():
        coef_down().wait_send()

    def finish(g, carry):
        @pl.when(has_high)
        def _():
            halo_up(g).wait_send()

        @pl.when(has_low)
        def _():
            halo_down(g).wait_send()

        own_copy(g).wait()
        for i in order:
            all_copy(g, i).wait_send()
            source = lax.rem(t + groups - i, groups)
            pltpu.make_async_remote_copy(
                src_ref=packed.at[g, source],
                dst_ref=cells_out.at[pl.ds(source * species_here + g * GROUP, GROUP)],
                send_sem=all_send.at[g, i - 1],
                recv_sem=all_recv.at[g, i - 1],
                device_id=(s, source),
                device_id_type=MESH,
            ).wait_recv()
        return carry

    lax.fori_loop(0, n_groups, finish, 0)
    rate_copy.wait()


def chemistry_kernel(reactions, table, cells, rates, lit, out, *scratch):
    made, lost_a, lost_b, middle = scratch[0:2], scratch[2:4], scratch[4:6], scratch[6]
    species = cells.shape[0] // 8
    zero = jnp.zeros((8, 128), F32)
    sums = (*made, *lost_a, *lost_b)
    at8 = lambda i: pl.ds(pl.multiple_of(i, 8), 8)
    day = lit[...]
    steps = (1.0 - 0.5 * day, 0.5 * day)

    def clear(i, carry):
        for j in range(8):
            for ref in sums:
                ref[at8(i * 64 + j * 8), :] = zero
        return carry

    lax.fori_loop(0, species // 8, clear, 0)
    for number in range(DAY_STEPS):
        source = cells if number == 0 else middle
        target = middle if number == 0 else out
        h = steps[number]

        def react(i, carry):
            for j in range(0, 16, 2):
                new = []
                for k in range(2):
                    r = i * 16 + j + k
                    a, b, p = at8(table[r]), at8(table[reactions + r]), at8(table[2 * reactions + r])
                    rate = rates[at8(r * 8), :]
                    ca, cb = source[a, :], source[b, :]
                    by_a = rate * cb
                    new.append((made[k], p, made[k][p, :] + by_a * ca))
                    new.append((lost_a[k], a, lost_a[k][a, :] + by_a))
                    new.append((lost_b[k], b, lost_b[k][b, :] + rate * ca))
                for ref, where, value in new:
                    ref[where, :] = value
            return carry

        lax.fori_loop(0, reactions // 16, react, 0)

        def update(i, carry):
            for j in range(8):
                o = at8(i * 64 + j * 8)
                gain = made[0][o, :] + made[1][o, :]
                loss = (lost_a[0][o, :] + lost_a[1][o, :]) + (lost_b[0][o, :] + lost_b[1][o, :])
                target[o, :] = (source[o, :] + h * gain) / (1.0 + h * loss)
                if number < DAY_STEPS - 1:
                    for ref in sums:
                        ref[o, :] = zero
            return carry

        lax.fori_loop(0, species // 8, update, 0)


def body(
    strips,
    groups,
    mixing_ratio_field,
    eastward_face_cfl,
    northward_face_cfl,
    upward_face_cfl,
    thermal_anomaly,
    radiant_flux,
    daylight_mask,
    baseline_kinetic_coefficient,
    arrhenius_barrier,
    photodissociation_factor,
    stoichiometry_table,
):
    species_here, levels, rows, width = mixing_ratio_field.shape
    species = species_here * groups
    reactions = baseline_kinetic_coefficient.shape[0]
    n_groups = species_here // GROUP

    def eight(x):
        return x.reshape(2, 2, 2, 128).transpose(0, 2, 1, 3).reshape(8, 128)

    lit = jnp.broadcast_to(
        daylight_mask.transpose(0, 2, 1).reshape(8, 1).astype(F32), (8, 128)
    )
    vmem = pl.BlockSpec(memory_space=pltpu.VMEM)
    smem = pl.BlockSpec(memory_space=pltpu.SMEM)
    anywhere = pl.BlockSpec(memory_space=pl.ANY)
    dma = pltpu.SemaphoreType.DMA
    cells, rates = pl.pallas_call(
        functools.partial(transport_kernel, strips, groups),
        out_shape=(
            jax.ShapeDtypeStruct((species, 8, 128), F32),
            jax.ShapeDtypeStruct((reactions, 8, 128), F32),
        ),
        in_specs=[anywhere, vmem, vmem, vmem, vmem, vmem, smem, smem, smem],
        out_specs=(anywhere, anywhere),
        scratch_shapes=[
            pltpu.VMEM((2, species_here, 2, rows, 128), F32),
            pltpu.VMEM((n_groups, rows + LOW + HIGH, 2, 2, GROUP, 128), F32),
            pltpu.VMEM((rows + 6, 2, 2, GROUP, 128), F32),
            pltpu.VMEM((rows + 3, 2, 2, GROUP, 128), F32),
            pltpu.VMEM((groups, 8, GROUP, 128), F32),
            pltpu.VMEM((n_groups, groups, GROUP, 8, 128), F32),
            pltpu.VMEM((6, rows + 7, 2, 2, GROUP, 128), F32),
            pltpu.VMEM((3, 2, 2, rows, 128), F32),
            pltpu.VMEM((3, 2, 8, 128), F32),
            pltpu.VMEM((3, 2, 8, 128), F32),
            pltpu.VMEM((3, 2, 8, 128), F32),
            pltpu.VMEM((3, 2, 8, 128), F32),
            pltpu.VMEM((reactions, 8, 128), F32),
            dma((n_groups, 2)),
            dma((2, n_groups)),
            dma((2, n_groups)),
            dma((2,)),
            dma((2,)),
            dma((n_groups, groups - 1)),
            dma((n_groups, groups - 1)),
            dma((n_groups,)),
            dma,
        ],
        compiler_params=pltpu.CompilerParams(
            collective_id=0, has_side_effects=True, vmem_limit_bytes=24 << 20
        ),
        name="transport",
    )(
        mixing_ratio_field,
        eastward_face_cfl,
        northward_face_cfl,
        upward_face_cfl,
        eight(thermal_anomaly),
        eight(radiant_flux) * lit,
        baseline_kinetic_coefficient,
        arrhenius_barrier,
        photodissociation_factor,
    )
    out = pl.pallas_call(
        functools.partial(chemistry_kernel, reactions),
        out_shape=jax.ShapeDtypeStruct((species * 8, 128), F32),
        in_specs=[smem, vmem, vmem, vmem],
        out_specs=vmem,
        scratch_shapes=[pltpu.VMEM((species * 8, 128), F32)] * 7,
        compiler_params=pltpu.CompilerParams(vmem_limit_bytes=24 << 20),
        name="chemistry",
    )(
        (stoichiometry_table * 8).reshape(3 * reactions),
        cells.reshape(species * 8, 128),
        rates.reshape(reactions * 8, 128),
        lit,
    )
    return out.reshape(species, 2, 2, 2, 128).transpose(0, 1, 3, 2, 4).reshape(species, 2, 2, 256)


def solution(mesh):
    placed = (
        P("tracer", None, "space", None),
        P(None, "space", None),
        P(None, "space", None),
        P(None, "space", None),
        P(None, ("space", "tracer"), None),
        P(None, ("space", "tracer"), None),
        P(None, ("space", "tracer"), None),
        P(),
        P(),
        P(),
        P(),
    )
    return jax.shard_map(
        functools.partial(body, mesh.shape["space"], mesh.shape["tracer"]),
        mesh=mesh,
        in_specs=placed,
        out_specs=P(None, None, ("space", "tracer"), None),
        check_vma=False,
    )
```

```python
import functools

import jax
import jax.numpy as jnp
from jax import lax
from jax.experimental import pallas as pl
from jax.experimental.pallas import tpu as pltpu
from jax.sharding import PartitionSpec as P

MESH = pl.DeviceIdType.MESH
F32 = jnp.float32

SECTIONS = 3
DAY_STEPS = 2
LOW, HIGH = 2 * SECTIONS, SECTIONS
UNROLL = 11
VMEM_BYTES = 60 << 20
CHUNKS = 6
PIECES = 4
GROUP = 8


def minmod(a, b):
    return jnp.maximum(jnp.minimum(a, jnp.maximum(b, 0.0)), jnp.minimum(b, 0.0))


def transport_kernel(
    strips,
    groups,
    field,
    ux,
    uy,
    uz,
    warm,
    glow,
    mask,
    base,
    barrier_coef,
    photo,
    stoichiometry,
    cells_out,
    rates_out,
    table_out,
    lit_out,
    raw,
    first,
    second,
    third,
    turned,
    packed,
    coef,
    plain,
    edge_up,
    edge_down,
    got_low,
    got_high,
    rates,
    sky,
    mask_here,
    coefs,
    species_of,
    table,
    load_sem,
    plain_sem,
    small_sem,
    halo_send,
    halo_recv,
    edge_send,
    edge_recv,
    all_send,
    all_recv,
    own_sem,
    rate_sem,
):
    s = lax.axis_index("space")
    t = lax.axis_index("tracer")
    n_groups = first.shape[0]
    rows = 16
    species_here = n_groups * GROUP
    has_low = s > 0
    has_high = s < strips - 1
    low, high = s - 1, s + 1

    def load(g, blk):
        return pltpu.make_async_copy(
            field.at[pl.ds(g * GROUP, GROUP), :, :, pl.ds(blk * 128, 128)],
            raw.at[blk, pl.ds(g * GROUP, GROUP)],
            load_sem.at[g, blk],
        )

    for g in range(n_groups):
        for blk in range(2):
            load(g, blk).start()

    plain_in = [
        pltpu.make_async_copy(
            u.at[:, :, pl.ds(blk * 128, 128)], plain.at[q, blk], plain_sem.at[q, blk]
        )
        for q, u in enumerate((ux, uy, uz))
        for blk in range(2)
    ]
    small_in = [
        pltpu.make_async_copy(source, target, small_sem.at[i])
        for i, (source, target) in enumerate(
            (
                (warm, sky.at[0]),
                (glow, sky.at[1]),
                (mask, mask_here),
                (stoichiometry, species_of),
                (base, coefs.at[pl.ds(0, base.shape[0])]),
                (barrier_coef, coefs.at[pl.ds(1024, base.shape[0])]),
                (photo, coefs.at[pl.ds(2048, base.shape[0])]),
            )
        )
    ]
    for copy in plain_in + small_in:
        copy.start()

    door = pltpu.get_barrier_semaphore()
    for i in range(1, groups):
        pl.semaphore_signal(
            door, inc=1, device_id=(s, lax.rem(t + i, groups)), device_id_type=MESH
        )

    @pl.when(has_low)
    def _():
        pl.semaphore_signal(door, inc=1, device_id=(low, t), device_id_type=MESH)

    @pl.when(has_high)
    def _():
        pl.semaphore_signal(door, inc=1, device_id=(high, t), device_id_type=MESH)

    for copy in plain_in:
        copy.wait()
    for q in range(3):
        for blk in range(2):
            for l in range(2):
                edge_up[q, blk, l * 4 : l * 4 + 4] = plain[q, blk, l, rows - 4 : rows]
                edge_down[q, blk, l * 4 : l * 4 + 4] = plain[q, blk, l, 0:4]

    flat = raw.reshape(2 * species_here * 2 * rows, 128)

    def turn(g, row):
        for l in range(2):
            for blk in range(2):
                start = blk * (species_here * 2 * rows) + g * (GROUP * 2 * rows) + l * rows + row
                first[g, row + LOW, l, blk] = flat[pl.ds(start, GROUP, stride=2 * rows), :]

    pl.semaphore_wait(door, groups - 1 + jnp.where(has_low, 1, 0) + jnp.where(has_high, 1, 0))

    def halo_up(g):
        return pltpu.make_async_remote_copy(
            src_ref=first.at[g, pl.ds(rows, LOW)],
            dst_ref=first.at[g, pl.ds(0, LOW)],
            send_sem=halo_send.at[0, g],
            recv_sem=halo_recv.at[0, g],
            device_id=(high, t),
            device_id_type=MESH,
        )

    def halo_down(g):
        return pltpu.make_async_remote_copy(
            src_ref=first.at[g, pl.ds(LOW, HIGH)],
            dst_ref=first.at[g, pl.ds(LOW + rows, HIGH)],
            send_sem=halo_send.at[1, g],
            recv_sem=halo_recv.at[1, g],
            device_id=(low, t),
            device_id_type=MESH,
        )

    def coef_up():
        return pltpu.make_async_remote_copy(
            src_ref=edge_up,
            dst_ref=got_low,
            send_sem=edge_send.at[0],
            recv_sem=edge_recv.at[0],
            device_id=(high, t),
            device_id_type=MESH,
        )

    def coef_down():
        return pltpu.make_async_remote_copy(
            src_ref=edge_down,
            dst_ref=got_high,
            send_sem=edge_send.at[1],
            recv_sem=edge_recv.at[1],
            device_id=(low, t),
            device_id_type=MESH,
        )

    @pl.when(has_high)
    def _():
        coef_up().start()

    @pl.when(has_low)
    def _():
        coef_down().start()

    def send_edges(g, carry):
        load(g, 0).wait()
        load(g, 1).wait()
        for row in range(rows - LOW, rows):
            turn(g, row)

        @pl.when(has_high)
        def _():
            halo_up(g).start()

        for row in range(HIGH):
            turn(g, row)

        @pl.when(has_low)
        def _():
            halo_down(g).start()

        return carry

    lax.fori_loop(0, n_groups, send_edges, 0)

    def turn_rest(g, carry):
        for row in range(HIGH, rows - LOW):
            turn(g, row)
        return carry

    lax.fori_loop(0, n_groups, turn_rest, 0)

    zero = jnp.zeros((GROUP, 128), F32)

    @pl.when(jnp.logical_not(has_low))
    def _():
        for g in range(n_groups):
            for row in range(LOW):
                for l in range(2):
                    for blk in range(2):
                        first[g, row, l, blk] = zero
        for q in range(3):
            for blk in range(2):
                got_low[q, blk] = zero

    @pl.when(jnp.logical_not(has_high))
    def _():
        for g in range(n_groups):
            for row in range(HIGH):
                for l in range(2):
                    for blk in range(2):
                        first[g, LOW + rows + row, l, blk] = zero
        for q in range(3):
            for blk in range(2):
                got_high[q, blk] = zero

    lane = lax.broadcasted_iota(jnp.int32, (GROUP, 128), 1)
    is_first = lane == 0
    is_last = lane == 127

    def from_left(x0, x1):
        r0, r1 = pltpu.roll(x0, 1, 1), pltpu.roll(x1, 1, 1)
        return jnp.where(is_first, r1, r0), jnp.where(is_first, r0, r1)

    def from_right(x0, x1):
        r0, r1 = pltpu.roll(x0, 127, 1), pltpu.roll(x1, 127, 1)
        return jnp.where(is_last, r1, r0), jnp.where(is_last, r0, r1)

    def spread(row, get):
        for l in range(2):
            for q in range(3):
                pair = [jnp.broadcast_to(get(q, l, blk), (GROUP, 128)) for blk in range(2)]
                if q == 1:
                    pair = from_right(*pair)
                for blk in range(2):
                    coef[2 * q, row, l, blk] = pair[blk]
                    coef[2 * q + 1, row, l, blk] = 0.5 * (1.0 - pair[blk])

    def spread_own(row, carry):
        spread(row + 4, lambda q, l, blk: plain[q, blk, l, pl.ds(row, 1), :])
        return carry

    lax.fori_loop(0, rows, spread_own, 0)

    @pl.when(has_low)
    def _():
        coef_up().wait_recv()

    @pl.when(has_high)
    def _():
        coef_down().wait_recv()

    for i in range(4):
        spread(i, lambda q, l, blk: got_low[q, blk, l * 4 + i : l * 4 + i + 1])
    for i in range(3):
        spread(rows + 4 + i, lambda q, l, blk: got_high[q, blk, l * 4 + i : l * 4 + i + 1])

    four = [(l, blk) for l in range(2) for blk in range(2)]

    def one_step(read, lo, count, write):
        state = []
        for l, blk in four:
            c0, c1, c2 = read(lo - 2, l, blk), read(lo - 1, l, blk), read(lo, l, blk)
            d1, d2 = c1 - c0, c2 - c1
            flux = coef[0, lo + 4, l, blk] * (c1 + coef[1, lo + 4, l, blk] * minmod(d1, d2))
            state += [c2, d2, flux]

        def body(i, state):
            row = i + lo
            after, swept = [], []
            for n, (l, blk) in enumerate(four):
                c, d, flux = state[3 * n : 3 * n + 3]
                c_next = read(row + 1, l, blk)
                d_next = c_next - c
                flux_next = coef[0, row + 5, l, blk] * (
                    c + coef[1, row + 5, l, blk] * minmod(d, d_next)
                )
                swept.append(c - (flux_next - flux))
                after += [c_next, d_next, flux_next]
            for l in range(2):
                c0, c1 = swept[2 * l], swept[2 * l + 1]
                m0, m1 = from_left(c0, c1)
                d0, d1 = c0 - m0, c1 - m1
                e0, e1 = from_right(d0, d1)
                g0 = coef[2, row + 4, l, 0] * (c0 + coef[3, row + 4, l, 0] * minmod(d0, e0))
                g1 = coef[2, row + 4, l, 1] * (c1 + coef[3, row + 4, l, 1] * minmod(d1, e1))
                h0, h1 = from_left(g0, g1)
                swept[2 * l] = c0 - (g0 - h0)
                swept[2 * l + 1] = c1 - (g1 - h1)
            for blk in range(2):
                c0, c1 = swept[blk], swept[2 + blk]
                rise = c1 - c0
                g0 = coef[4, row + 4, 0, blk] * (c0 + coef[5, row + 4, 0, blk] * minmod(c0, rise))
                g1 = coef[4, row + 4, 1, blk] * (c1 + coef[5, row + 4, 1, blk] * minmod(rise, -c1))
                write(row, 0, blk, c0 - g0)
                write(row, 1, blk, c1 - (g1 - g0))
            return tuple(after)

        def several(n, state):
            for j in range(UNROLL):
                state = body(n * UNROLL + j, state)
            return state

        state = lax.fori_loop(0, count // UNROLL, several, tuple(state))
        for j in range(count - count % UNROLL, count):
            state = body(j, state)

    def all_copy(g, i):
        to = lax.rem(t + i, groups)
        return pltpu.make_async_remote_copy(
            src_ref=packed.at[g, to],
            dst_ref=cells_out.at[pl.ds(t * species_here + g * GROUP, GROUP)],
            send_sem=all_send.at[g, i - 1],
            recv_sem=all_recv.at[g, i - 1],
            device_id=(s, to),
            device_id_type=MESH,
        )

    def own_copy(g):
        return pltpu.make_async_copy(
            packed.at[g, t],
            cells_out.at[pl.ds(t * species_here + g * GROUP, GROUP)],
            own_sem.at[g],
        )

    turned_flat = turned.reshape(groups * 8 * GROUP, 128)
    order = [i for i in range(1, groups) if i % 2 == 1] + [i for i in range(1, groups) if i % 2 == 0]

    def sweep_group(g, carry):
        @pl.when(has_low)
        def _():
            halo_up(g).wait_recv()

        @pl.when(has_high)
        def _():
            halo_down(g).wait_recv()

        def put2(row, l, blk, v):
            second[row + 4, l, blk] = v

        def put3(row, l, blk, v):
            third[row + 2, l, blk] = v

        def put4(row, l, blk, v):
            turned[row // 2, l * 4 + blk * 2 + row % 2] = v

        one_step(lambda row, l, blk: first[g, row + LOW, l, blk], -4, rows + 6, put2)
        one_step(lambda row, l, blk: second[row + 4, l, blk], -2, rows + 3, put3)
        one_step(lambda row, l, blk: third[row + 2, l, blk], 0, rows, put4)

        def pack(to, carry):
            for k in range(GROUP):
                packed[g, to, k] = turned_flat[pl.ds(to * (8 * GROUP) + k, 8, stride=GROUP), :]
            return carry

        lax.fori_loop(0, groups, pack, 0)
        for i in order:
            all_copy(g, i).start()
        own_copy(g).start()
        return carry

    lax.fori_loop(0, n_groups, sweep_group, 0)

    for copy in small_in:
        copy.wait()
    for l in range(2):
        for blk in range(2):
            lit_out[l * 4 + blk * 2 : l * 4 + blk * 2 + 2, :] = jnp.broadcast_to(
                mask_here[l, :, blk : blk + 1].astype(F32), (2, 128)
            )
    cold = 1.0 - sky[0]
    light = sky[1] * lit_out[...]
    reactions = rates.shape[0]
    for q in range(3):
        for j in range(reactions // 128):
            n = q * (reactions // 128) + j
            table[n : n + 1, :] = species_of[q : q + 1, j * 128 : j * 128 + 128] * 8

    def rate(i, carry):
        for j in range(8):
            r = i * 8 + j
            rates[r] = coefs[r] * jnp.exp(coefs[1024 + r] * cold) + coefs[2048 + r] * light
        return carry

    lax.fori_loop(0, reactions // 8, rate, 0)
    rate_copy = pltpu.make_async_copy(rates, rates_out, rate_sem.at[0])
    rate_copy.start()
    table_copy = pltpu.make_async_copy(table, table_out, rate_sem.at[1])
    table_copy.start()

    @pl.when(has_high)
    def _():
        coef_up().wait_send()

    @pl.when(has_low)
    def _():
        coef_down().wait_send()

    def finish(g, carry):
        @pl.when(has_high)
        def _():
            halo_up(g).wait_send()

        @pl.when(has_low)
        def _():
            halo_down(g).wait_send()

        own_copy(g).wait()
        for i in order:
            all_copy(g, i).wait_send()
            source = lax.rem(t + groups - i, groups)
            pltpu.make_async_remote_copy(
                src_ref=packed.at[g, source],
                dst_ref=cells_out.at[pl.ds(source * species_here + g * GROUP, GROUP)],
                send_sem=all_send.at[g, i - 1],
                recv_sem=all_recv.at[g, i - 1],
                device_id=(s, source),
                device_id_type=MESH,
            ).wait_recv()
        return carry

    lax.fori_loop(0, n_groups, finish, 0)
    rate_copy.wait()
    table_copy.wait()


def chemistry_kernel(
    reactions,
    table_in,
    cells_in,
    rates_in,
    lit_in,
    out,
    table,
    cells,
    rates,
    lit,
    result,
    made_0,
    made_1,
    lost_a0,
    lost_a1,
    lost_b0,
    lost_b1,
    middle,
    first_sem,
    rate_sem,
    out_sem,
):
    made, lost_a, lost_b = (made_0, made_1), (lost_a0, lost_a1), (lost_b0, lost_b1)
    species = cells.shape[0] // 8
    zero = jnp.zeros((8, 128), F32)
    sums = (*made, *lost_a, *lost_b)
    at8 = lambda i: pl.ds(pl.multiple_of(i, 8), 8)
    first_in = [
        pltpu.make_async_copy(source, target, first_sem.at[i])
        for i, (source, target) in enumerate(((cells_in, cells), (table_in, table), (lit_in, lit)))
    ]
    part = reactions // CHUNKS

    def rates_piece(i):
        where = pl.ds(pl.multiple_of(i * part * 8, 8), part * 8)
        return pltpu.make_async_copy(rates_in.at[where, :], rates.at[where, :], rate_sem.at[i])

    for copy in first_in:
        copy.start()
    for i in range(CHUNKS):
        rates_piece(i).start()

    def clear(i, carry):
        for j in range(8):
            for ref in sums:
                ref[at8(i * 64 + j * 8), :] = zero
        return carry

    lax.fori_loop(0, species // 8, clear, 0)
    for copy in first_in:
        copy.wait()
    day = lit[...]
    steps = (1.0 - 0.5 * day, 0.5 * day)
    piece = species // PIECES

    def out_piece(i):
        where = pl.ds(pl.multiple_of(i * piece * 8, 8), piece * 8)
        return pltpu.make_async_copy(result.at[where, :], out.at[where, :], out_sem.at[i])

    for number in range(DAY_STEPS):
        last = number == DAY_STEPS - 1
        source = cells if number == 0 else middle
        target = result if last else middle
        h = steps[number]

        def react(i, carry):
            for j in range(0, 16, 2):
                new = []
                for k in range(2):
                    r = i * 16 + j + k
                    a, b, p = at8(table[r]), at8(table[reactions + r]), at8(table[2 * reactions + r])
                    rate = rates[at8(r * 8), :]
                    ca, cb = source[a, :], source[b, :]
                    by_a = rate * cb
                    new.append((made[k], p, made[k][p, :] + by_a * ca))
                    new.append((lost_a[k], a, lost_a[k][a, :] + by_a))
                    new.append((lost_b[k], b, lost_b[k][b, :] + rate * ca))
                for ref, where, value in new:
                    ref[where, :] = value
            return carry

        if number == 0:

            def react_chunk(i, carry):
                rates_piece(i).wait()
                return lax.fori_loop(i * (part // 16), (i + 1) * (part // 16), react, carry)

            lax.fori_loop(0, CHUNKS, react_chunk, 0)
        else:
            lax.fori_loop(0, reactions // 16, react, 0)

        def update(i, carry):
            for j in range(8):
                o = at8(i * 64 + j * 8)
                gain = made[0][o, :] + made[1][o, :]
                loss = (lost_a[0][o, :] + lost_a[1][o, :]) + (lost_b[0][o, :] + lost_b[1][o, :])
                target[o, :] = (source[o, :] + h * gain) / (1.0 + h * loss)
                if not last:
                    for ref in sums:
                        ref[o, :] = zero
            return carry

        def update_piece(i, carry):
            lax.fori_loop(i * (piece // 8), (i + 1) * (piece // 8), update, 0)
            out_piece(i).start()
            return carry

        if last:
            lax.fori_loop(0, PIECES, update_piece, 0)
        else:
            lax.fori_loop(0, species // 8, update, 0)
    for i in range(PIECES):
        out_piece(i).wait()


def body(
    strips,
    groups,
    mixing_ratio_field,
    eastward_face_cfl,
    northward_face_cfl,
    upward_face_cfl,
    thermal_anomaly,
    radiant_flux,
    daylight_mask,
    baseline_kinetic_coefficient,
    arrhenius_barrier,
    photodissociation_factor,
    stoichiometry_table,
):
    species_here, levels, rows, width = mixing_ratio_field.shape
    species = species_here * groups
    reactions = baseline_kinetic_coefficient.shape[0]
    n_groups = species_here // GROUP

    def eight(x):
        return x.reshape(2, 2, 2, 128).transpose(0, 2, 1, 3).reshape(8, 128)

    vmem = pl.BlockSpec(memory_space=pltpu.VMEM)
    hbm = pl.BlockSpec(memory_space=pltpu.HBM)
    dma = pltpu.SemaphoreType.DMA
    cells, rates, table, lit = pl.pallas_call(
        functools.partial(transport_kernel, strips, groups),
        out_shape=(
            jax.ShapeDtypeStruct((species, 8, 128), F32),
            jax.ShapeDtypeStruct((reactions, 8, 128), F32),
            jax.ShapeDtypeStruct((24, 128), jnp.int32),
            jax.ShapeDtypeStruct((8, 128), F32),
        ),
        in_specs=[hbm] * 11,
        out_specs=(hbm, hbm, hbm, vmem),
        scratch_shapes=[
            pltpu.VMEM((2, species_here, 2, rows, 128), F32),
            pltpu.VMEM((n_groups, rows + LOW + HIGH, 2, 2, GROUP, 128), F32),
            pltpu.VMEM((rows + 6, 2, 2, GROUP, 128), F32),
            pltpu.VMEM((rows + 3, 2, 2, GROUP, 128), F32),
            pltpu.VMEM((groups, 8, GROUP, 128), F32),
            pltpu.VMEM((n_groups, groups, GROUP, 8, 128), F32),
            pltpu.VMEM((6, rows + 7, 2, 2, GROUP, 128), F32),
            pltpu.VMEM((3, 2, 2, rows, 128), F32),
            pltpu.VMEM((3, 2, 8, 128), F32),
            pltpu.VMEM((3, 2, 8, 128), F32),
            pltpu.VMEM((3, 2, 8, 128), F32),
            pltpu.VMEM((3, 2, 8, 128), F32),
            pltpu.VMEM((reactions, 8, 128), F32),
            pltpu.VMEM((2, 8, 128), F32),
            pltpu.VMEM((2, 2, 2), jnp.int32),
            pltpu.SMEM((3 * 1024,), F32),
            pltpu.VMEM((3, reactions), jnp.int32),
            pltpu.VMEM((24, 128), jnp.int32),
            dma((n_groups, 2)),
            dma((3, 2)),
            dma((7,)),
            dma((2, n_groups)),
            dma((2, n_groups)),
            dma((2,)),
            dma((2,)),
            dma((n_groups, groups - 1)),
            dma((n_groups, groups - 1)),
            dma((n_groups,)),
            dma((2,)),
        ],
        compiler_params=pltpu.CompilerParams(
            collective_id=0, has_side_effects=True, vmem_limit_bytes=VMEM_BYTES
        ),
        name="transport",
    )(
        mixing_ratio_field,
        eastward_face_cfl,
        northward_face_cfl,
        upward_face_cfl,
        eight(thermal_anomaly),
        eight(radiant_flux),
        daylight_mask,
        baseline_kinetic_coefficient,
        arrhenius_barrier,
        photodissociation_factor,
        stoichiometry_table,
    )
    out = pl.pallas_call(
        functools.partial(chemistry_kernel, reactions),
        out_shape=jax.ShapeDtypeStruct((species * 8, 128), F32),
        in_specs=[hbm] * 4,
        out_specs=hbm,
        scratch_shapes=[
            pltpu.SMEM((24 * 128,), jnp.int32),
            pltpu.VMEM((species * 8, 128), F32),
            pltpu.VMEM((reactions * 8, 128), F32),
            pltpu.VMEM((8, 128), F32),
        ]
        + [pltpu.VMEM((species * 8, 128), F32)] * 8
        + [dma((3,)), dma((CHUNKS,)), dma((PIECES,))],
        compiler_params=pltpu.CompilerParams(vmem_limit_bytes=VMEM_BYTES),
        name="chemistry",
    )(
        table.reshape(24 * 128),
        cells.reshape(species * 8, 128),
        rates.reshape(reactions * 8, 128),
        lit,
    )
    return out.reshape(species, 2, 2, 2, 128).transpose(0, 1, 3, 2, 4).reshape(species, 2, 2, 256)


def solution(mesh):
    placed = (
        P("tracer", None, "space", None),
        P(None, "space", None),
        P(None, "space", None),
        P(None, "space", None),
        P(None, ("space", "tracer"), None),
        P(None, ("space", "tracer"), None),
        P(None, ("space", "tracer"), None),
        P(),
        P(),
        P(),
        P(),
    )
    return jax.shard_map(
        functools.partial(body, mesh.shape["space"], mesh.shape["tracer"]),
        mesh=mesh,
        in_specs=placed,
        out_specs=P(None, None, ("space", "tracer"), None),
        check_vma=False,
    )
```

```python
import functools

import jax
import jax.numpy as jnp
from jax import lax
from jax.experimental import pallas as pl
from jax.experimental.pallas import tpu as pltpu
from jax.sharding import PartitionSpec as P

MESH = pl.DeviceIdType.MESH
F32 = jnp.float32

SECTIONS = 3
DAY_STEPS = 2
LOW, HIGH = 2 * SECTIONS, SECTIONS
UNROLL = 8
VMEM_BYTES = 60 << 20
ROUND = 4
CHUNKS = 4
PIECES = 4
GROUP = 8


def minmod(a, b):
    return jnp.maximum(jnp.minimum(a, jnp.maximum(b, 0.0)), jnp.minimum(b, 0.0))


def transport_kernel(
    strips,
    groups,
    field,
    ux,
    uy,
    uz,
    warm,
    glow,
    mask,
    base,
    barrier_coef,
    photo,
    stoichiometry,
    cells_out,
    rates_out,
    table_out,
    lit_out,
    raw,
    first,
    second,
    third,
    packed,
    coef,
    plain,
    edge_up,
    edge_down,
    got_low,
    got_high,
    rates,
    sky,
    mask_here,
    coefs,
    species_of,
    table,
    load_sem,
    plain_sem,
    small_sem,
    halo_send,
    halo_recv,
    edge_send,
    edge_recv,
    all_send,
    all_recv,
    own_sem,
    rate_sem,
):
    s = lax.axis_index("space")
    t = lax.axis_index("tracer")
    n_groups = first.shape[0]
    rows = 16
    species_here = n_groups * GROUP
    has_low = s > 0
    has_high = s < strips - 1
    low, high = s - 1, s + 1

    def load(g, blk):
        return pltpu.make_async_copy(
            field.at[pl.ds(g * GROUP, GROUP), :, :, pl.ds(blk * 128, 128)],
            raw.at[blk, pl.ds(g * GROUP, GROUP)],
            load_sem.at[g, blk],
        )

    for g in range(n_groups):
        for blk in range(2):
            load(g, blk).start()

    plain_in = [
        pltpu.make_async_copy(
            u.at[:, :, pl.ds(blk * 128, 128)], plain.at[q, blk], plain_sem.at[q, blk]
        )
        for q, u in enumerate((ux, uy, uz))
        for blk in range(2)
    ]
    small_in = [
        pltpu.make_async_copy(source, target, small_sem.at[i])
        for i, (source, target) in enumerate(
            (
                (warm, sky.at[0]),
                (glow, sky.at[1]),
                (mask, mask_here),
                (stoichiometry, species_of),
                (base, coefs.at[pl.ds(0, base.shape[0])]),
                (barrier_coef, coefs.at[pl.ds(1024, base.shape[0])]),
                (photo, coefs.at[pl.ds(2048, base.shape[0])]),
            )
        )
    ]
    for copy in plain_in + small_in:
        copy.start()

    door = pltpu.get_barrier_semaphore()
    for i in range(1, groups):
        pl.semaphore_signal(
            door, inc=1, device_id=(s, lax.rem(t + i, groups)), device_id_type=MESH
        )

    @pl.when(has_low)
    def _():
        pl.semaphore_signal(door, inc=1, device_id=(low, t), device_id_type=MESH)

    @pl.when(has_high)
    def _():
        pl.semaphore_signal(door, inc=1, device_id=(high, t), device_id_type=MESH)

    for copy in plain_in:
        copy.wait()
    for q in range(3):
        for blk in range(2):
            for l in range(2):
                edge_up[q, blk, l * 4 : l * 4 + 4] = plain[q, blk, l, rows - 4 : rows]
                edge_down[q, blk, l * 4 : l * 4 + 4] = plain[q, blk, l, 0:4]

    flat = raw.reshape(2 * species_here * 2 * rows, 128)

    def turn(g, row):
        for l in range(2):
            for blk in range(2):
                start = blk * (species_here * 2 * rows) + g * (GROUP * 2 * rows) + l * rows + row
                first[g, row + LOW, l, blk] = flat[pl.ds(start, GROUP, stride=2 * rows), :]

    pl.semaphore_wait(door, groups - 1 + jnp.where(has_low, 1, 0) + jnp.where(has_high, 1, 0))

    def halo_up(g):
        return pltpu.make_async_remote_copy(
            src_ref=first.at[g, pl.ds(rows, LOW)],
            dst_ref=first.at[g, pl.ds(0, LOW)],
            send_sem=halo_send.at[0, g],
            recv_sem=halo_recv.at[0, g],
            device_id=(high, t),
            device_id_type=MESH,
        )

    def halo_down(g):
        return pltpu.make_async_remote_copy(
            src_ref=first.at[g, pl.ds(LOW, HIGH)],
            dst_ref=first.at[g, pl.ds(LOW + rows, HIGH)],
            send_sem=halo_send.at[1, g],
            recv_sem=halo_recv.at[1, g],
            device_id=(low, t),
            device_id_type=MESH,
        )

    def coef_up():
        return pltpu.make_async_remote_copy(
            src_ref=edge_up,
            dst_ref=got_low,
            send_sem=edge_send.at[0],
            recv_sem=edge_recv.at[0],
            device_id=(high, t),
            device_id_type=MESH,
        )

    def coef_down():
        return pltpu.make_async_remote_copy(
            src_ref=edge_down,
            dst_ref=got_high,
            send_sem=edge_send.at[1],
            recv_sem=edge_recv.at[1],
            device_id=(low, t),
            device_id_type=MESH,
        )

    @pl.when(has_high)
    def _():
        coef_up().start()

    @pl.when(has_low)
    def _():
        coef_down().start()

    def send_edges(g, carry):
        load(g, 0).wait()
        load(g, 1).wait()
        for row in range(rows - LOW, rows):
            turn(g, row)

        @pl.when(has_high)
        def _():
            halo_up(g).start()

        for row in range(HIGH):
            turn(g, row)

        @pl.when(has_low)
        def _():
            halo_down(g).start()

        return carry

    lax.fori_loop(0, n_groups, send_edges, 0)

    def turn_rest(g, carry):
        for row in range(HIGH, rows - LOW):
            turn(g, row)
        return carry

    lax.fori_loop(0, n_groups, turn_rest, 0)

    zero = jnp.zeros((GROUP, 128), F32)

    @pl.when(jnp.logical_not(has_low))
    def _():
        for g in range(n_groups):
            for row in range(LOW):
                for l in range(2):
                    for blk in range(2):
                        first[g, row, l, blk] = zero
        for q in range(3):
            for blk in range(2):
                got_low[q, blk] = zero

    @pl.when(jnp.logical_not(has_high))
    def _():
        for g in range(n_groups):
            for row in range(HIGH):
                for l in range(2):
                    for blk in range(2):
                        first[g, LOW + rows + row, l, blk] = zero
        for q in range(3):
            for blk in range(2):
                got_high[q, blk] = zero

    lane = lax.broadcasted_iota(jnp.int32, (GROUP, 128), 1)
    is_first = lane == 0
    is_last = lane == 127

    def from_left(x0, x1):
        r0, r1 = pltpu.roll(x0, 1, 1), pltpu.roll(x1, 1, 1)
        return jnp.where(is_first, r1, r0), jnp.where(is_first, r0, r1)

    def from_right(x0, x1):
        r0, r1 = pltpu.roll(x0, 127, 1), pltpu.roll(x1, 127, 1)
        return jnp.where(is_last, r1, r0), jnp.where(is_last, r0, r1)

    def spread(row, get):
        for l in range(2):
            for q in range(3):
                pair = [jnp.broadcast_to(get(q, l, blk), (GROUP, 128)) for blk in range(2)]
                if q == 1:
                    pair = from_right(*pair)
                for blk in range(2):
                    coef[2 * q, row, l, blk] = pair[blk]
                    coef[2 * q + 1, row, l, blk] = 0.5 * (1.0 - pair[blk])

    def spread_own(row, carry):
        spread(row + 4, lambda q, l, blk: plain[q, blk, l, pl.ds(row, 1), :])
        return carry

    lax.fori_loop(0, rows, spread_own, 0)

    @pl.when(has_low)
    def _():
        coef_up().wait_recv()

    @pl.when(has_high)
    def _():
        coef_down().wait_recv()

    for i in range(4):
        spread(i, lambda q, l, blk: got_low[q, blk, l * 4 + i : l * 4 + i + 1])
    for i in range(3):
        spread(rows + 4 + i, lambda q, l, blk: got_high[q, blk, l * 4 + i : l * 4 + i + 1])

    four = [(l, blk) for l in range(2) for blk in range(2)]

    def one_step(read, lo, count, write):
        state = []
        for l, blk in four:
            c0, c1, c2 = read(lo - 2, l, blk), read(lo - 1, l, blk), read(lo, l, blk)
            d1, d2 = c1 - c0, c2 - c1
            flux = coef[0, lo + 4, l, blk] * (c1 + coef[1, lo + 4, l, blk] * minmod(d1, d2))
            state += [c2, d2, flux]

        def body(i, state):
            row = i + lo
            after, swept = [], []
            for n, (l, blk) in enumerate(four):
                c, d, flux = state[3 * n : 3 * n + 3]
                c_next = read(row + 1, l, blk)
                d_next = c_next - c
                flux_next = coef[0, row + 5, l, blk] * (
                    c + coef[1, row + 5, l, blk] * minmod(d, d_next)
                )
                swept.append(c - (flux_next - flux))
                after += [c_next, d_next, flux_next]
            for l in range(2):
                c0, c1 = swept[2 * l], swept[2 * l + 1]
                m0, m1 = from_left(c0, c1)
                d0, d1 = c0 - m0, c1 - m1
                e0, e1 = from_right(d0, d1)
                g0 = coef[2, row + 4, l, 0] * (c0 + coef[3, row + 4, l, 0] * minmod(d0, e0))
                g1 = coef[2, row + 4, l, 1] * (c1 + coef[3, row + 4, l, 1] * minmod(d1, e1))
                h0, h1 = from_left(g0, g1)
                swept[2 * l] = c0 - (g0 - h0)
                swept[2 * l + 1] = c1 - (g1 - h1)
            for blk in range(2):
                c0, c1 = swept[blk], swept[2 + blk]
                rise = c1 - c0
                g0 = coef[4, row + 4, 0, blk] * (c0 + coef[5, row + 4, 0, blk] * minmod(c0, rise))
                g1 = coef[4, row + 4, 1, blk] * (c1 + coef[5, row + 4, 1, blk] * minmod(rise, -c1))
                write(row, 0, blk, c0 - g0)
                write(row, 1, blk, c1 - (g1 - g0))
            return tuple(after)

        def several(n, state):
            for j in range(UNROLL):
                state = body(n * UNROLL + j, state)
            return state

        state = lax.fori_loop(0, count // UNROLL, several, tuple(state))
        for j in range(count - count % UNROLL, count):
            state = body(j, state)

    def all_copy(g, i):
        to = lax.rem(t + i, groups)
        return pltpu.make_async_remote_copy(
            src_ref=packed.at[g, to],
            dst_ref=cells_out.at[pl.ds(t * species_here + g * GROUP, GROUP)],
            send_sem=all_send.at[g, i - 1],
            recv_sem=all_recv.at[g, i - 1],
            device_id=(s, to),
            device_id_type=MESH,
        )

    def own_copy(g):
        return pltpu.make_async_copy(
            packed.at[g, t],
            cells_out.at[pl.ds(t * species_here + g * GROUP, GROUP)],
            own_sem.at[g],
        )

    packed_flat = packed.reshape(n_groups * groups * GROUP * 8, 128)
    order = [i for i in range(1, groups) if i % 2 == 1] + [i for i in range(1, groups) if i % 2 == 0]

    def halos_gone(g, carry):
        @pl.when(has_high)
        def _():
            halo_up(g).wait_send()

        @pl.when(has_low)
        def _():
            halo_down(g).wait_send()

        return carry

    def sweep_group(g, carry):
        @pl.when(has_low)
        def _():
            halo_up(g).wait_recv()

        @pl.when(has_high)
        def _():
            halo_down(g).wait_recv()

        def put2(row, l, blk, v):
            second[row + 4, l, blk] = v

        def put3(row, l, blk, v):
            third[row + 2, l, blk] = v

        def put4(row, l, blk, v):
            start = (g * groups + row // 2) * (GROUP * 8) + l * 4 + blk * 2 + row % 2
            packed_flat[pl.ds(start, GROUP, stride=8), :] = v

        one_step(lambda row, l, blk: first[g, row + LOW, l, blk], -4, rows + 6, put2)
        one_step(lambda row, l, blk: second[row + 4, l, blk], -2, rows + 3, put3)
        one_step(lambda row, l, blk: third[row + 2, l, blk], 0, rows, put4)

        @pl.when(g == 0)
        def _():
            lax.fori_loop(0, n_groups, halos_gone, 0)

        for i in order:
            all_copy(g, i).start()
        own_copy(g).start()
        return carry

    lax.fori_loop(0, n_groups, sweep_group, 0)

    for copy in small_in:
        copy.wait()
    for l in range(2):
        for blk in range(2):
            lit_out[l * 4 + blk * 2 : l * 4 + blk * 2 + 2, :] = jnp.broadcast_to(
                mask_here[l, :, blk : blk + 1].astype(F32), (2, 128)
            )
    cold = 1.0 - sky[0]
    light = sky[1] * lit_out[...]
    reactions = rates.shape[0]
    for q in range(3):
        for j in range(reactions // 128):
            n = q * (reactions // 128) + j
            table[n : n + 1, :] = species_of[q : q + 1, j * 128 : j * 128 + 128] * 8

    ways = reactions // 128

    def rate(i, carry):
        for j in range(2):
            for w in range(ways):
                r = w * 128 + 2 * i + j
                rates[(2 * i + j) * ways + w] = (
                    coefs[r] * jnp.exp(coefs[1024 + r] * cold) + coefs[2048 + r] * light
                )
        return carry

    lax.fori_loop(0, 128 // 2, rate, 0)
    rate_copy = pltpu.make_async_copy(rates, rates_out, rate_sem.at[0])
    rate_copy.start()
    table_copy = pltpu.make_async_copy(table, table_out, rate_sem.at[1])
    table_copy.start()

    @pl.when(has_high)
    def _():
        coef_up().wait_send()

    @pl.when(has_low)
    def _():
        coef_down().wait_send()

    def finish(g, carry):
        own_copy(g).wait()
        for i in order:
            all_copy(g, i).wait_send()
            source = lax.rem(t + groups - i, groups)
            pltpu.make_async_remote_copy(
                src_ref=packed.at[g, source],
                dst_ref=cells_out.at[pl.ds(source * species_here + g * GROUP, GROUP)],
                send_sem=all_send.at[g, i - 1],
                recv_sem=all_recv.at[g, i - 1],
                device_id=(s, source),
                device_id_type=MESH,
            ).wait_recv()
        return carry

    lax.fori_loop(0, n_groups, finish, 0)
    rate_copy.wait()
    table_copy.wait()


def chemistry_kernel(ways, table_in, cells_in, rates_in, lit_in, out, *scratch):
    cells, rates, lit, result, middle = scratch[:5]
    sums = scratch[5 : 5 + 6 * DAY_STEPS]
    table = scratch[5 + 6 * DAY_STEPS : 5 + 6 * DAY_STEPS + 3 * ways]
    first_sem, table_sem, rate_sem, out_sem = scratch[-4:]
    species = cells.shape[0] // 8
    zero = jnp.zeros((8, 128), F32)
    at8 = lambda i: pl.ds(pl.multiple_of(i, 8), 8)
    first_in = [
        pltpu.make_async_copy(source, target, first_sem.at[i])
        for i, (source, target) in enumerate(((cells_in, cells), (lit_in, lit)))
    ] + [
        pltpu.make_async_copy(table_in.at[pl.ds(n * 128, 128)], table[n], table_sem.at[n])
        for n in range(3 * ways)
    ]
    part = 128 // CHUNKS

    def rates_piece(i):
        where = pl.ds(pl.multiple_of(i * part * ways * 8, 8), part * ways * 8)
        return pltpu.make_async_copy(rates_in.at[where, :], rates.at[where, :], rate_sem.at[i])

    for copy in first_in:
        copy.start()
    for i in range(CHUNKS):
        rates_piece(i).start()

    def clear(i, carry):
        for j in range(4):
            for ref in sums:
                ref[at8(i * 32 + j * 8), :] = zero
        return carry

    lax.fori_loop(0, species // 4, clear, 0)
    for copy in first_in:
        copy.wait()
    day = lit[...]
    steps = (1.0 - 0.5 * day, 0.5 * day)
    piece = species // PIECES

    def out_piece(i):
        where = pl.ds(pl.multiple_of(i * piece * 8, 8), piece * 8)
        return pltpu.make_async_copy(result.at[where, :], out.at[where, :], out_sem.at[i])

    for number in range(DAY_STEPS):
        last = number == DAY_STEPS - 1
        source = cells if number == 0 else middle
        target = result if last else middle
        h = steps[number]
        made, lost_a, lost_b = (sums[6 * number + 2 * n : 6 * number + 2 * n + 2] for n in range(3))

        def react(n, carry):
            for j in range(ROUND):
                i = n * ROUND + j
                for w in range(0, ways, 2):
                    new = []
                    for k in range(2):
                        a, b, p = (at8(table[q * ways + w + k][i]) for q in range(3))
                        rate = rates[at8(n * (ROUND * ways * 8) + (j * ways + w + k) * 8), :]
                        ca, cb = source[a, :], source[b, :]
                        by_a = rate * cb
                        new.append((made[k], p, made[k][p, :] + by_a * ca))
                        new.append((lost_a[k], a, lost_a[k][a, :] + by_a))
                        new.append((lost_b[k], b, lost_b[k][b, :] + rate * ca))
                    for ref, where, value in new:
                        ref[where, :] = value
            return carry

        if number == 0:

            def react_chunk(i, carry):
                rates_piece(i).wait()
                return lax.fori_loop(i * (part // ROUND), (i + 1) * (part // ROUND), react, carry)

            lax.fori_loop(0, CHUNKS, react_chunk, 0)
        else:
            lax.fori_loop(0, 128 // ROUND, react, 0)

        def update(i, carry):
            for j in range(8):
                o = at8(i * 64 + j * 8)
                gain = made[0][o, :] + made[1][o, :]
                loss = (lost_a[0][o, :] + lost_a[1][o, :]) + (lost_b[0][o, :] + lost_b[1][o, :])
                target[o, :] = (source[o, :] + h * gain) / (1.0 + h * loss)
            return carry

        def update_piece(i, carry):
            lax.fori_loop(i * (piece // 8), (i + 1) * (piece // 8), update, 0)
            out_piece(i).start()
            return carry

        if last:
            lax.fori_loop(0, PIECES, update_piece, 0)
        else:
            lax.fori_loop(0, species // 8, update, 0)
    for i in range(PIECES):
        out_piece(i).wait()


def body(
    strips,
    groups,
    mixing_ratio_field,
    eastward_face_cfl,
    northward_face_cfl,
    upward_face_cfl,
    thermal_anomaly,
    radiant_flux,
    daylight_mask,
    baseline_kinetic_coefficient,
    arrhenius_barrier,
    photodissociation_factor,
    stoichiometry_table,
):
    species_here, levels, rows, width = mixing_ratio_field.shape
    species = species_here * groups
    reactions = baseline_kinetic_coefficient.shape[0]
    n_groups = species_here // GROUP

    def eight(x):
        return x.reshape(2, 2, 2, 128).transpose(0, 2, 1, 3).reshape(8, 128)

    vmem = pl.BlockSpec(memory_space=pltpu.VMEM)
    hbm = pl.BlockSpec(memory_space=pltpu.HBM)
    dma = pltpu.SemaphoreType.DMA
    cells, rates, table, lit = pl.pallas_call(
        functools.partial(transport_kernel, strips, groups),
        out_shape=(
            jax.ShapeDtypeStruct((species, 8, 128), F32),
            jax.ShapeDtypeStruct((reactions, 8, 128), F32),
            jax.ShapeDtypeStruct((24, 128), jnp.int32),
            jax.ShapeDtypeStruct((8, 128), F32),
        ),
        in_specs=[hbm] * 11,
        out_specs=(hbm, hbm, hbm, vmem),
        scratch_shapes=[
            pltpu.VMEM((2, species_here, 2, rows, 128), F32),
            pltpu.VMEM((n_groups, rows + LOW + HIGH, 2, 2, GROUP, 128), F32),
            pltpu.VMEM((rows + 6, 2, 2, GROUP, 128), F32),
            pltpu.VMEM((rows + 3, 2, 2, GROUP, 128), F32),
            pltpu.VMEM((n_groups, groups, GROUP, 8, 128), F32),
            pltpu.VMEM((6, rows + 7, 2, 2, GROUP, 128), F32),
            pltpu.VMEM((3, 2, 2, rows, 128), F32),
            pltpu.VMEM((3, 2, 8, 128), F32),
            pltpu.VMEM((3, 2, 8, 128), F32),
            pltpu.VMEM((3, 2, 8, 128), F32),
            pltpu.VMEM((3, 2, 8, 128), F32),
            pltpu.VMEM((reactions, 8, 128), F32),
            pltpu.VMEM((2, 8, 128), F32),
            pltpu.VMEM((2, 2, 2), jnp.int32),
            pltpu.SMEM((3 * 1024,), F32),
            pltpu.VMEM((3, reactions), jnp.int32),
            pltpu.VMEM((24, 128), jnp.int32),
            dma((n_groups, 2)),
            dma((3, 2)),
            dma((7,)),
            dma((2, n_groups)),
            dma((2, n_groups)),
            dma((2,)),
            dma((2,)),
            dma((n_groups, groups - 1)),
            dma((n_groups, groups - 1)),
            dma((n_groups,)),
            dma((2,)),
        ],
        compiler_params=pltpu.CompilerParams(
            collective_id=0, has_side_effects=True, vmem_limit_bytes=VMEM_BYTES
        ),
        name="transport",
    )(
        mixing_ratio_field,
        eastward_face_cfl,
        northward_face_cfl,
        upward_face_cfl,
        eight(thermal_anomaly),
        eight(radiant_flux),
        daylight_mask,
        baseline_kinetic_coefficient,
        arrhenius_barrier,
        photodissociation_factor,
        stoichiometry_table,
    )
    out = pl.pallas_call(
        functools.partial(chemistry_kernel, reactions // 128),
        out_shape=jax.ShapeDtypeStruct((species * 8, 128), F32),
        in_specs=[hbm] * 4,
        out_specs=hbm,
        scratch_shapes=[
            pltpu.VMEM((species * 8, 128), F32),
            pltpu.VMEM((reactions * 8, 128), F32),
            pltpu.VMEM((8, 128), F32),
        ]
        + [pltpu.VMEM((species * 8, 128), F32)] * (2 + 6 * DAY_STEPS)
        + [pltpu.SMEM((128,), jnp.int32)] * (3 * (reactions // 128))
        + [dma((2,)), dma((3 * (reactions // 128),)), dma((CHUNKS,)), dma((PIECES,))],
        compiler_params=pltpu.CompilerParams(vmem_limit_bytes=VMEM_BYTES),
        name="chemistry",
    )(
        table.reshape(24 * 128),
        cells.reshape(species * 8, 128),
        rates.reshape(reactions * 8, 128),
        lit,
    )
    return out.reshape(species, 2, 2, 2, 128).transpose(0, 1, 3, 2, 4).reshape(species, 2, 2, 256)


def solution(mesh):
    placed = (
        P("tracer", None, "space", None),
        P(None, "space", None),
        P(None, "space", None),
        P(None, "space", None),
        P(None, ("space", "tracer"), None),
        P(None, ("space", "tracer"), None),
        P(None, ("space", "tracer"), None),
        P(),
        P(),
        P(),
        P(),
    )
    return jax.shard_map(
        functools.partial(body, mesh.shape["space"], mesh.shape["tracer"]),
        mesh=mesh,
        in_specs=placed,
        out_specs=P(None, None, ("space", "tracer"), None),
        check_vma=False,
    )
```

```python
import functools

import jax
import jax.numpy as jnp
from jax import lax
from jax.experimental import pallas as pl
from jax.experimental.pallas import tpu as pltpu
from jax.sharding import PartitionSpec as P

MESH = pl.DeviceIdType.MESH
F32 = jnp.float32

SECTIONS = 3
DAY_STEPS = 2
LOW, HIGH = 2 * SECTIONS, SECTIONS
UNROLL = 8
VMEM_BYTES = 60 << 20
ROUND = 8
CHUNKS = 4
PIECES = 8
GROUP = 8


def minmod(a, b):
    return jnp.maximum(jnp.minimum(a, jnp.maximum(b, 0.0)), jnp.minimum(b, 0.0))


def transport_kernel(
    strips,
    groups,
    field,
    ux,
    uy,
    uz,
    warm,
    glow,
    mask,
    base,
    barrier_coef,
    photo,
    stoichiometry,
    cells_out,
    rates_out,
    table_out,
    lit_out,
    raw,
    first,
    second,
    third,
    packed,
    coef,
    plain,
    edge_up,
    edge_down,
    got_low,
    got_high,
    rates,
    sky,
    mask_here,
    coefs,
    species_of,
    table,
    load_sem,
    plain_sem,
    small_sem,
    halo_send,
    halo_recv,
    edge_send,
    edge_recv,
    all_send,
    all_recv,
    own_sem,
    rate_sem,
):
    s = lax.axis_index("space")
    t = lax.axis_index("tracer")
    n_groups = first.shape[0]
    rows = 16
    species_here = n_groups * GROUP
    has_low = s > 0
    has_high = s < strips - 1
    low, high = s - 1, s + 1

    def load(g, blk):
        return pltpu.make_async_copy(
            field.at[pl.ds(g * GROUP, GROUP), :, :, pl.ds(blk * 128, 128)],
            raw.at[blk, pl.ds(g * GROUP, GROUP)],
            load_sem.at[g, blk],
        )

    for g in range(n_groups):
        for blk in range(2):
            load(g, blk).start()

    plain_in = [
        pltpu.make_async_copy(
            u.at[:, :, pl.ds(blk * 128, 128)], plain.at[q, blk], plain_sem.at[q, blk]
        )
        for q, u in enumerate((ux, uy, uz))
        for blk in range(2)
    ]
    small_in = [
        pltpu.make_async_copy(source, target, small_sem.at[i])
        for i, (source, target) in enumerate(
            (
                (warm, sky.at[0]),
                (glow, sky.at[1]),
                (mask, mask_here),
                (stoichiometry, species_of),
                (base, coefs.at[pl.ds(0, base.shape[0])]),
                (barrier_coef, coefs.at[pl.ds(1024, base.shape[0])]),
                (photo, coefs.at[pl.ds(2048, base.shape[0])]),
            )
        )
    ]
    for copy in plain_in + small_in:
        copy.start()

    door = pltpu.get_barrier_semaphore()
    for i in range(1, groups):
        pl.semaphore_signal(
            door, inc=1, device_id=(s, lax.rem(t + i, groups)), device_id_type=MESH
        )

    @pl.when(has_low)
    def _():
        pl.semaphore_signal(door, inc=1, device_id=(low, t), device_id_type=MESH)

    @pl.when(has_high)
    def _():
        pl.semaphore_signal(door, inc=1, device_id=(high, t), device_id_type=MESH)

    for copy in plain_in:
        copy.wait()
    for q in range(3):
        for blk in range(2):
            for l in range(2):
                edge_up[q, blk, l * 4 : l * 4 + 4] = plain[q, blk, l, rows - 4 : rows]
                edge_down[q, blk, l * 4 : l * 4 + 4] = plain[q, blk, l, 0:4]

    flat = raw.reshape(2 * species_here * 2 * rows, 128)

    def turn(g, row):
        for l in range(2):
            for blk in range(2):
                start = blk * (species_here * 2 * rows) + g * (GROUP * 2 * rows) + l * rows + row
                first[g, row + LOW, l, blk] = flat[pl.ds(start, GROUP, stride=2 * rows), :]

    def halo_up(g):
        return pltpu.make_async_remote_copy(
            src_ref=first.at[g, pl.ds(rows, LOW)],
            dst_ref=first.at[g, pl.ds(0, LOW)],
            send_sem=halo_send.at[0, g],
            recv_sem=halo_recv.at[0, g],
            device_id=(high, t),
            device_id_type=MESH,
        )

    def halo_down(g):
        return pltpu.make_async_remote_copy(
            src_ref=first.at[g, pl.ds(LOW, HIGH)],
            dst_ref=first.at[g, pl.ds(LOW + rows, HIGH)],
            send_sem=halo_send.at[1, g],
            recv_sem=halo_recv.at[1, g],
            device_id=(low, t),
            device_id_type=MESH,
        )

    def coef_up():
        return pltpu.make_async_remote_copy(
            src_ref=edge_up,
            dst_ref=got_low,
            send_sem=edge_send.at[0],
            recv_sem=edge_recv.at[0],
            device_id=(high, t),
            device_id_type=MESH,
        )

    def coef_down():
        return pltpu.make_async_remote_copy(
            src_ref=edge_down,
            dst_ref=got_high,
            send_sem=edge_send.at[1],
            recv_sem=edge_recv.at[1],
            device_id=(low, t),
            device_id_type=MESH,
        )

    def turn_edges(g, carry):
        load(g, 0).wait()
        load(g, 1).wait()
        for row in (*range(HIGH), *range(rows - LOW, rows)):
            turn(g, row)
        return carry

    lax.fori_loop(0, n_groups, turn_edges, 0)

    pl.semaphore_wait(door, groups - 1 + jnp.where(has_low, 1, 0) + jnp.where(has_high, 1, 0))

    @pl.when(has_high)
    def _():
        coef_up().start()

    @pl.when(has_low)
    def _():
        coef_down().start()

    def send_edges(g, carry):
        @pl.when(has_low)
        def _():
            halo_down(g).start()

        @pl.when(has_high)
        def _():
            halo_up(g).start()

        return carry

    lax.fori_loop(0, n_groups, send_edges, 0)

    def turn_rest(g, carry):
        for row in range(HIGH, rows - LOW):
            turn(g, row)
        return carry

    lax.fori_loop(0, n_groups, turn_rest, 0)

    zero = jnp.zeros((GROUP, 128), F32)

    @pl.when(jnp.logical_not(has_low))
    def _():
        for g in range(n_groups):
            for row in range(LOW):
                for l in range(2):
                    for blk in range(2):
                        first[g, row, l, blk] = zero
        for q in range(3):
            for blk in range(2):
                got_low[q, blk] = zero

    @pl.when(jnp.logical_not(has_high))
    def _():
        for g in range(n_groups):
            for row in range(HIGH):
                for l in range(2):
                    for blk in range(2):
                        first[g, LOW + rows + row, l, blk] = zero
        for q in range(3):
            for blk in range(2):
                got_high[q, blk] = zero

    lane = lax.broadcasted_iota(jnp.int32, (GROUP, 128), 1)
    is_first = lane == 0
    is_last = lane == 127

    def from_left(x0, x1):
        r0, r1 = pltpu.roll(x0, 1, 1), pltpu.roll(x1, 1, 1)
        return jnp.where(is_first, r1, r0), jnp.where(is_first, r0, r1)

    def from_right(x0, x1):
        r0, r1 = pltpu.roll(x0, 127, 1), pltpu.roll(x1, 127, 1)
        return jnp.where(is_last, r1, r0), jnp.where(is_last, r0, r1)

    def spread(row, get):
        for l in range(2):
            for q in range(3):
                pair = [jnp.broadcast_to(get(q, l, blk), (GROUP, 128)) for blk in range(2)]
                if q == 1:
                    pair = from_right(*pair)
                for blk in range(2):
                    coef[2 * q, row, l, blk] = pair[blk]
                    coef[2 * q + 1, row, l, blk] = 0.5 * (1.0 - pair[blk])

    def spread_own(row, carry):
        spread(row + 4, lambda q, l, blk: plain[q, blk, l, pl.ds(row, 1), :])
        return carry

    lax.fori_loop(0, rows, spread_own, 0)

    @pl.when(has_low)
    def _():
        coef_up().wait_recv()

    @pl.when(has_high)
    def _():
        coef_down().wait_recv()

    for i in range(4):
        spread(i, lambda q, l, blk: got_low[q, blk, l * 4 + i : l * 4 + i + 1])
    for i in range(3):
        spread(rows + 4 + i, lambda q, l, blk: got_high[q, blk, l * 4 + i : l * 4 + i + 1])

    four = [(l, blk) for l in range(2) for blk in range(2)]

    def one_step(read, lo, count, write):
        state = []
        for l, blk in four:
            c0, c1, c2 = read(lo - 2, l, blk), read(lo - 1, l, blk), read(lo, l, blk)
            d1, d2 = c1 - c0, c2 - c1
            flux = coef[0, lo + 4, l, blk] * (c1 + coef[1, lo + 4, l, blk] * minmod(d1, d2))
            state += [c2, d2, flux]

        def body(i, state):
            row = i + lo
            after, swept = [], []
            for n, (l, blk) in enumerate(four):
                c, d, flux = state[3 * n : 3 * n + 3]
                c_next = read(row + 1, l, blk)
                d_next = c_next - c
                flux_next = coef[0, row + 5, l, blk] * (
                    c + coef[1, row + 5, l, blk] * minmod(d, d_next)
                )
                swept.append(c - (flux_next - flux))
                after += [c_next, d_next, flux_next]
            for l in range(2):
                c0, c1 = swept[2 * l], swept[2 * l + 1]
                m0, m1 = from_left(c0, c1)
                d0, d1 = c0 - m0, c1 - m1
                e0, e1 = from_right(d0, d1)
                g0 = coef[2, row + 4, l, 0] * (c0 + coef[3, row + 4, l, 0] * minmod(d0, e0))
                g1 = coef[2, row + 4, l, 1] * (c1 + coef[3, row + 4, l, 1] * minmod(d1, e1))
                h0, h1 = from_left(g0, g1)
                swept[2 * l] = c0 - (g0 - h0)
                swept[2 * l + 1] = c1 - (g1 - h1)
            for blk in range(2):
                c0, c1 = swept[blk], swept[2 + blk]
                rise = c1 - c0
                g0 = coef[4, row + 4, 0, blk] * (c0 + coef[5, row + 4, 0, blk] * minmod(c0, rise))
                g1 = coef[4, row + 4, 1, blk] * (c1 + coef[5, row + 4, 1, blk] * minmod(rise, -c1))
                write(row, 0, blk, c0 - g0)
                write(row, 1, blk, c1 - (g1 - g0))
            return tuple(after)

        def several(n, state):
            for j in range(UNROLL):
                state = body(n * UNROLL + j, state)
            return state

        state = lax.fori_loop(0, count // UNROLL, several, tuple(state))
        for j in range(count - count % UNROLL, count):
            state = body(j, state)

    def all_copy(g, i):
        to = lax.rem(t + i, groups)
        return pltpu.make_async_remote_copy(
            src_ref=packed.at[g, to],
            dst_ref=cells_out.at[pl.ds(t * species_here + g * GROUP, GROUP)],
            send_sem=all_send.at[g, i - 1],
            recv_sem=all_recv.at[g, i - 1],
            device_id=(s, to),
            device_id_type=MESH,
        )

    def own_copy(g):
        return pltpu.make_async_copy(
            packed.at[g, t],
            cells_out.at[pl.ds(t * species_here + g * GROUP, GROUP)],
            own_sem.at[g],
        )

    packed_flat = packed.reshape(n_groups * groups * GROUP * 8, 128)
    order = [i for i in range(1, groups) if i % 2 == 1] + [i for i in range(1, groups) if i % 2 == 0]

    def halos_gone(g, carry):
        @pl.when(has_high)
        def _():
            halo_up(g).wait_send()

        @pl.when(has_low)
        def _():
            halo_down(g).wait_send()

        return carry

    def sweep_group(g, carry):
        @pl.when(has_low)
        def _():
            halo_up(g).wait_recv()

        @pl.when(has_high)
        def _():
            halo_down(g).wait_recv()

        def put2(row, l, blk, v):
            second[row + 4, l, blk] = v

        def put3(row, l, blk, v):
            third[row + 2, l, blk] = v

        def put4(row, l, blk, v):
            start = (g * groups + row // 2) * (GROUP * 8) + l * 4 + blk * 2 + row % 2
            packed_flat[pl.ds(start, GROUP, stride=8), :] = v

        one_step(lambda row, l, blk: first[g, row + LOW, l, blk], -4, rows + 6, put2)
        one_step(lambda row, l, blk: second[row + 4, l, blk], -2, rows + 3, put3)
        one_step(lambda row, l, blk: third[row + 2, l, blk], 0, rows, put4)

        @pl.when(g == 0)
        def _():
            lax.fori_loop(0, n_groups, halos_gone, 0)

        for i in order:
            all_copy(g, i).start()
        own_copy(g).start()
        return carry

    lax.fori_loop(0, n_groups, sweep_group, 0)

    for copy in small_in:
        copy.wait()
    for l in range(2):
        for blk in range(2):
            lit_out[l * 4 + blk * 2 : l * 4 + blk * 2 + 2, :] = jnp.broadcast_to(
                mask_here[l, :, blk : blk + 1].astype(F32), (2, 128)
            )
    cold = 1.0 - sky[0]
    light = sky[1] * lit_out[...]
    reactions = rates.shape[0]
    for q in range(3):
        for j in range(reactions // 128):
            n = q * (reactions // 128) + j
            table[n : n + 1, :] = species_of[q : q + 1, j * 128 : j * 128 + 128] * 8

    ways = reactions // 128

    def rate(i, carry):
        for j in range(2):
            for w in range(ways):
                r = w * 128 + 2 * i + j
                rates[(2 * i + j) * ways + w] = (
                    coefs[r] * jnp.exp(coefs[1024 + r] * cold) + coefs[2048 + r] * light
                )
        return carry

    lax.fori_loop(0, 128 // 2, rate, 0)
    rate_copy = pltpu.make_async_copy(rates, rates_out, rate_sem.at[0])
    rate_copy.start()
    table_copy = pltpu.make_async_copy(table, table_out, rate_sem.at[1])
    table_copy.start()

    @pl.when(has_high)
    def _():
        coef_up().wait_send()

    @pl.when(has_low)
    def _():
        coef_down().wait_send()

    def finish(g, carry):
        own_copy(g).wait()
        for i in order:
            all_copy(g, i).wait_send()
            source = lax.rem(t + groups - i, groups)
            pltpu.make_async_remote_copy(
                src_ref=packed.at[g, source],
                dst_ref=cells_out.at[pl.ds(source * species_here + g * GROUP, GROUP)],
                send_sem=all_send.at[g, i - 1],
                recv_sem=all_recv.at[g, i - 1],
                device_id=(s, source),
                device_id_type=MESH,
            ).wait_recv()
        return carry

    lax.fori_loop(0, n_groups, finish, 0)
    rate_copy.wait()
    table_copy.wait()


def chemistry_kernel(ways, table_in, cells_in, rates_in, lit_in, out, *scratch):
    cells, rates, lit, result, middle = scratch[:5]
    sums = scratch[5 : 5 + 6 * DAY_STEPS]
    table = scratch[5 + 6 * DAY_STEPS : 5 + 6 * DAY_STEPS + 3 * ways]
    first_sem, table_sem, rate_sem, out_sem = scratch[-4:]
    species = cells.shape[0] // 8
    zero = jnp.zeros((8, 128), F32)
    at8 = lambda i: pl.ds(pl.multiple_of(i, 8), 8)
    first_in = [
        pltpu.make_async_copy(source, target, first_sem.at[i])
        for i, (source, target) in enumerate(((cells_in, cells), (lit_in, lit)))
    ] + [
        pltpu.make_async_copy(table_in.at[pl.ds(n * 128, 128)], table[n], table_sem.at[n])
        for n in range(3 * ways)
    ]
    part = 128 // CHUNKS

    def rates_piece(i):
        where = pl.ds(pl.multiple_of(i * part * ways * 8, 8), part * ways * 8)
        return pltpu.make_async_copy(rates_in.at[where, :], rates.at[where, :], rate_sem.at[i])

    for copy in first_in:
        copy.start()
    for i in range(CHUNKS):
        rates_piece(i).start()

    def clear(i, carry):
        for j in range(4):
            for ref in sums:
                ref[at8(i * 32 + j * 8), :] = zero
        return carry

    lax.fori_loop(0, species // 4, clear, 0)
    for copy in first_in:
        copy.wait()
    day = lit[...]
    steps = (1.0 - 0.5 * day, 0.5 * day)
    piece = species // PIECES

    def out_piece(i):
        where = pl.ds(pl.multiple_of(i * piece * 8, 8), piece * 8)
        return pltpu.make_async_copy(result.at[where, :], out.at[where, :], out_sem.at[i])

    for number in range(DAY_STEPS):
        last = number == DAY_STEPS - 1
        source = cells if number == 0 else middle
        target = result if last else middle
        h = steps[number]
        made, lost_a, lost_b = (sums[6 * number + 2 * n : 6 * number + 2 * n + 2] for n in range(3))

        def react(n, carry):
            for j in range(ROUND):
                i = n * ROUND + j
                for w in range(0, ways, 2):
                    new = []
                    for k in range(2):
                        a, b, p = (at8(table[q * ways + w + k][i]) for q in range(3))
                        rate = rates[at8(n * (ROUND * ways * 8) + (j * ways + w + k) * 8), :]
                        ca, cb = source[a, :], source[b, :]
                        by_a = rate * cb
                        new.append((made[k], p, made[k][p, :] + by_a * ca))
                        new.append((lost_a[k], a, lost_a[k][a, :] + by_a))
                        new.append((lost_b[k], b, lost_b[k][b, :] + rate * ca))
                    for ref, where, value in new:
                        ref[where, :] = value
            return carry

        if number == 0:

            def react_chunk(i, carry):
                rates_piece(i).wait()
                return lax.fori_loop(i * (part // ROUND), (i + 1) * (part // ROUND), react, carry)

            lax.fori_loop(0, CHUNKS, react_chunk, 0)
        else:
            lax.fori_loop(0, 128 // ROUND, react, 0)

        def update(i, carry):
            for j in range(32):
                o = at8(i * 256 + j * 8)
                gain = made[0][o, :] + made[1][o, :]
                loss = (lost_a[0][o, :] + lost_a[1][o, :]) + (lost_b[0][o, :] + lost_b[1][o, :])
                target[o, :] = (source[o, :] + h * gain) / (1.0 + h * loss)
            return carry

        def update_piece(i, carry):
            lax.fori_loop(i * (piece // 32), (i + 1) * (piece // 32), update, 0)
            out_piece(i).start()
            return carry

        if last:
            lax.fori_loop(0, PIECES, update_piece, 0)
        else:
            lax.fori_loop(0, species // 32, update, 0)
    for i in range(PIECES):
        out_piece(i).wait()


def body(
    strips,
    groups,
    mixing_ratio_field,
    eastward_face_cfl,
    northward_face_cfl,
    upward_face_cfl,
    thermal_anomaly,
    radiant_flux,
    daylight_mask,
    baseline_kinetic_coefficient,
    arrhenius_barrier,
    photodissociation_factor,
    stoichiometry_table,
):
    species_here, levels, rows, width = mixing_ratio_field.shape
    species = species_here * groups
    reactions = baseline_kinetic_coefficient.shape[0]
    n_groups = species_here // GROUP

    def eight(x):
        return x.reshape(2, 2, 2, 128).transpose(0, 2, 1, 3).reshape(8, 128)

    vmem = pl.BlockSpec(memory_space=pltpu.VMEM)
    hbm = pl.BlockSpec(memory_space=pltpu.HBM)
    dma = pltpu.SemaphoreType.DMA
    cells, rates, table, lit = pl.pallas_call(
        functools.partial(transport_kernel, strips, groups),
        out_shape=(
            jax.ShapeDtypeStruct((species, 8, 128), F32),
            jax.ShapeDtypeStruct((reactions, 8, 128), F32),
            jax.ShapeDtypeStruct((24, 128), jnp.int32),
            jax.ShapeDtypeStruct((8, 128), F32),
        ),
        in_specs=[hbm] * 11,
        out_specs=(hbm, hbm, hbm, vmem),
        scratch_shapes=[
            pltpu.VMEM((2, species_here, 2, rows, 128), F32),
            pltpu.VMEM((n_groups, rows + LOW + HIGH, 2, 2, GROUP, 128), F32),
            pltpu.VMEM((rows + 6, 2, 2, GROUP, 128), F32),
            pltpu.VMEM((rows + 3, 2, 2, GROUP, 128), F32),
            pltpu.VMEM((n_groups, groups, GROUP, 8, 128), F32),
            pltpu.VMEM((6, rows + 7, 2, 2, GROUP, 128), F32),
            pltpu.VMEM((3, 2, 2, rows, 128), F32),
            pltpu.VMEM((3, 2, 8, 128), F32),
            pltpu.VMEM((3, 2, 8, 128), F32),
            pltpu.VMEM((3, 2, 8, 128), F32),
            pltpu.VMEM((3, 2, 8, 128), F32),
            pltpu.VMEM((reactions, 8, 128), F32),
            pltpu.VMEM((2, 8, 128), F32),
            pltpu.VMEM((2, 2, 2), jnp.int32),
            pltpu.SMEM((3 * 1024,), F32),
            pltpu.VMEM((3, reactions), jnp.int32),
            pltpu.VMEM((24, 128), jnp.int32),
            dma((n_groups, 2)),
            dma((3, 2)),
            dma((7,)),
            dma((2, n_groups)),
            dma((2, n_groups)),
            dma((2,)),
            dma((2,)),
            dma((n_groups, groups - 1)),
            dma((n_groups, groups - 1)),
            dma((n_groups,)),
            dma((2,)),
        ],
        compiler_params=pltpu.CompilerParams(
            collective_id=0, has_side_effects=True, vmem_limit_bytes=VMEM_BYTES
        ),
        name="transport",
    )(
        mixing_ratio_field,
        eastward_face_cfl,
        northward_face_cfl,
        upward_face_cfl,
        eight(thermal_anomaly),
        eight(radiant_flux),
        daylight_mask,
        baseline_kinetic_coefficient,
        arrhenius_barrier,
        photodissociation_factor,
        stoichiometry_table,
    )
    out = pl.pallas_call(
        functools.partial(chemistry_kernel, reactions // 128),
        out_shape=jax.ShapeDtypeStruct((species * 8, 128), F32),
        in_specs=[hbm] * 4,
        out_specs=hbm,
        scratch_shapes=[
            pltpu.VMEM((species * 8, 128), F32),
            pltpu.VMEM((reactions * 8, 128), F32),
            pltpu.VMEM((8, 128), F32),
        ]
        + [pltpu.VMEM((species * 8, 128), F32)] * (2 + 6 * DAY_STEPS)
        + [pltpu.SMEM((128,), jnp.int32)] * (3 * (reactions // 128))
        + [dma((2,)), dma((3 * (reactions // 128),)), dma((CHUNKS,)), dma((PIECES,))],
        compiler_params=pltpu.CompilerParams(vmem_limit_bytes=VMEM_BYTES),
        name="chemistry",
    )(
        table.reshape(24 * 128),
        cells.reshape(species * 8, 128),
        rates.reshape(reactions * 8, 128),
        lit,
    )
    return out.reshape(species, 2, 2, 2, 128).transpose(0, 1, 3, 2, 4).reshape(species, 2, 2, 256)


def solution(mesh):
    placed = (
        P("tracer", None, "space", None),
        P(None, "space", None),
        P(None, "space", None),
        P(None, "space", None),
        P(None, ("space", "tracer"), None),
        P(None, ("space", "tracer"), None),
        P(None, ("space", "tracer"), None),
        P(),
        P(),
        P(),
        P(),
    )
    return jax.shard_map(
        functools.partial(body, mesh.shape["space"], mesh.shape["tracer"]),
        mesh=mesh,
        in_specs=placed,
        out_specs=P(None, None, ("space", "tracer"), None),
        check_vma=False,
    )
```

```python
import functools

import jax
import jax.numpy as jnp
from jax import lax
from jax.experimental import pallas as pl
from jax.experimental.pallas import tpu as pltpu
from jax.sharding import PartitionSpec as P

MESH = pl.DeviceIdType.MESH
F32 = jnp.float32

SECTIONS = 3
DAY_STEPS = 2
LOW, HIGH = 2 * SECTIONS, SECTIONS
UNROLL = 8
VMEM_BYTES = 60 << 20
ROUND = 8
CHUNKS = 2
PIECES = 8
GROUP = 8


def minmod(a, b):
    return jnp.maximum(jnp.minimum(a, jnp.maximum(b, 0.0)), jnp.minimum(b, 0.0))


def transport_kernel(
    strips,
    groups,
    field,
    ux,
    uy,
    uz,
    warm,
    glow,
    mask,
    base,
    barrier_coef,
    photo,
    stoichiometry,
    cells_out,
    rates_out,
    table_out,
    lit_out,
    raw,
    first,
    second,
    third,
    packed,
    coef,
    plain,
    edge_up,
    edge_down,
    got_low,
    got_high,
    rates,
    sky,
    mask_here,
    coefs,
    species_of,
    table,
    load_sem,
    plain_sem,
    small_sem,
    halo_send,
    halo_recv,
    edge_send,
    edge_recv,
    all_send,
    all_recv,
    own_sem,
    rate_sem,
):
    s = lax.axis_index("space")
    t = lax.axis_index("tracer")
    n_groups = first.shape[0]
    rows = 16
    species_here = n_groups * GROUP
    has_low = s > 0
    has_high = s < strips - 1
    low, high = s - 1, s + 1

    def load(g, blk):
        return pltpu.make_async_copy(
            field.at[pl.ds(g * GROUP, GROUP), :, :, pl.ds(blk * 128, 128)],
            raw.at[blk, pl.ds(g * GROUP, GROUP)],
            load_sem.at[g, blk],
        )

    for g in range(n_groups):
        for blk in range(2):
            load(g, blk).start()

    plain_in = [
        pltpu.make_async_copy(
            u.at[:, :, pl.ds(blk * 128, 128)], plain.at[q, blk], plain_sem.at[q, blk]
        )
        for q, u in enumerate((ux, uy, uz))
        for blk in range(2)
    ]
    small_in = [
        pltpu.make_async_copy(source, target, small_sem.at[i])
        for i, (source, target) in enumerate(
            (
                (warm, sky.at[0]),
                (glow, sky.at[1]),
                (mask, mask_here),
                (stoichiometry, species_of),
                (base, coefs.at[pl.ds(0, base.shape[0])]),
                (barrier_coef, coefs.at[pl.ds(1024, base.shape[0])]),
                (photo, coefs.at[pl.ds(2048, base.shape[0])]),
            )
        )
    ]
    for copy in plain_in + small_in:
        copy.start()

    door = pltpu.get_barrier_semaphore()
    for i in range(1, groups):
        pl.semaphore_signal(
            door, inc=1, device_id=(s, lax.rem(t + i, groups)), device_id_type=MESH
        )

    @pl.when(has_low)
    def _():
        pl.semaphore_signal(door, inc=1, device_id=(low, t), device_id_type=MESH)

    @pl.when(has_high)
    def _():
        pl.semaphore_signal(door, inc=1, device_id=(high, t), device_id_type=MESH)

    for copy in plain_in:
        copy.wait()
    for q in range(3):
        for blk in range(2):
            for l in range(2):
                edge_up[q, blk, l * 4 : l * 4 + 4] = plain[q, blk, l, rows - 4 : rows]
                edge_down[q, blk, l * 4 : l * 4 + 4] = plain[q, blk, l, 0:4]

    flat = raw.reshape(2 * species_here * 2 * rows, 128)

    def turn(g, row):
        for l in range(2):
            for blk in range(2):
                start = blk * (species_here * 2 * rows) + g * (GROUP * 2 * rows) + l * rows + row
                first[g, row + LOW, l, blk] = flat[pl.ds(start, GROUP, stride=2 * rows), :]

    def halo_up(g):
        return pltpu.make_async_remote_copy(
            src_ref=first.at[g, pl.ds(rows, LOW)],
            dst_ref=first.at[g, pl.ds(0, LOW)],
            send_sem=halo_send.at[0, g],
            recv_sem=halo_recv.at[0, g],
            device_id=(high, t),
            device_id_type=MESH,
        )

    def halo_down(g):
        return pltpu.make_async_remote_copy(
            src_ref=first.at[g, pl.ds(LOW, HIGH)],
            dst_ref=first.at[g, pl.ds(LOW + rows, HIGH)],
            send_sem=halo_send.at[1, g],
            recv_sem=halo_recv.at[1, g],
            device_id=(low, t),
            device_id_type=MESH,
        )

    def coef_up():
        return pltpu.make_async_remote_copy(
            src_ref=edge_up,
            dst_ref=got_low,
            send_sem=edge_send.at[0],
            recv_sem=edge_recv.at[0],
            device_id=(high, t),
            device_id_type=MESH,
        )

    def coef_down():
        return pltpu.make_async_remote_copy(
            src_ref=edge_down,
            dst_ref=got_high,
            send_sem=edge_send.at[1],
            recv_sem=edge_recv.at[1],
            device_id=(low, t),
            device_id_type=MESH,
        )

    def turn_edges(g, carry):
        load(g, 0).wait()
        load(g, 1).wait()
        for row in (*range(HIGH), *range(rows - LOW, rows)):
            turn(g, row)
        return carry

    lax.fori_loop(0, n_groups, turn_edges, 0)

    pl.semaphore_wait(door, groups - 1 + jnp.where(has_low, 1, 0) + jnp.where(has_high, 1, 0))

    @pl.when(has_high)
    def _():
        coef_up().start()

    @pl.when(has_low)
    def _():
        coef_down().start()

    def send_up(g, carry):
        @pl.when(has_high)
        def _():
            halo_up(g).start()

        return carry

    lax.fori_loop(0, n_groups, send_up, 0)

    def send_down(g, carry):
        @pl.when(has_low)
        def _():
            halo_down(g).start()

        return carry

    lax.fori_loop(0, n_groups, send_down, 0)

    def turn_rest(g, carry):
        for row in range(HIGH, rows - LOW):
            turn(g, row)
        return carry

    lax.fori_loop(0, n_groups, turn_rest, 0)

    zero = jnp.zeros((GROUP, 128), F32)

    @pl.when(jnp.logical_not(has_low))
    def _():
        for g in range(n_groups):
            for row in range(LOW):
                for l in range(2):
                    for blk in range(2):
                        first[g, row, l, blk] = zero
        for q in range(3):
            for blk in range(2):
                got_low[q, blk] = zero

    @pl.when(jnp.logical_not(has_high))
    def _():
        for g in range(n_groups):
            for row in range(HIGH):
                for l in range(2):
                    for blk in range(2):
                        first[g, LOW + rows + row, l, blk] = zero
        for q in range(3):
            for blk in range(2):
                got_high[q, blk] = zero

    lane = lax.broadcasted_iota(jnp.int32, (GROUP, 128), 1)
    is_first = lane == 0
    is_last = lane == 127

    def from_left(x0, x1):
        r0, r1 = pltpu.roll(x0, 1, 1), pltpu.roll(x1, 1, 1)
        return jnp.where(is_first, r1, r0), jnp.where(is_first, r0, r1)

    def from_right(x0, x1):
        r0, r1 = pltpu.roll(x0, 127, 1), pltpu.roll(x1, 127, 1)
        return jnp.where(is_last, r1, r0), jnp.where(is_last, r0, r1)

    def spread(row, get):
        for l in range(2):
            for q in range(3):
                pair = [jnp.broadcast_to(get(q, l, blk), (GROUP, 128)) for blk in range(2)]
                if q == 1:
                    pair = from_right(*pair)
                for blk in range(2):
                    coef[2 * q, row, l, blk] = pair[blk]
                    coef[2 * q + 1, row, l, blk] = 0.5 * (1.0 - pair[blk])

    def spread_own(row, carry):
        spread(row + 4, lambda q, l, blk: plain[q, blk, l, pl.ds(row, 1), :])
        return carry

    lax.fori_loop(0, rows, spread_own, 0)

    @pl.when(has_low)
    def _():
        coef_up().wait_recv()

    @pl.when(has_high)
    def _():
        coef_down().wait_recv()

    for i in range(4):
        spread(i, lambda q, l, blk: got_low[q, blk, l * 4 + i : l * 4 + i + 1])
    for i in range(3):
        spread(rows + 4 + i, lambda q, l, blk: got_high[q, blk, l * 4 + i : l * 4 + i + 1])

    four = [(l, blk) for l in range(2) for blk in range(2)]

    def one_step(read, lo, count, write):
        state = []
        for l, blk in four:
            c0, c1, c2 = read(lo - 2, l, blk), read(lo - 1, l, blk), read(lo, l, blk)
            d1, d2 = c1 - c0, c2 - c1
            flux = coef[0, lo + 4, l, blk] * (c1 + coef[1, lo + 4, l, blk] * minmod(d1, d2))
            state += [c2, d2, flux]

        def body(i, state):
            row = i + lo
            after, swept = [], []
            for n, (l, blk) in enumerate(four):
                c, d, flux = state[3 * n : 3 * n + 3]
                c_next = read(row + 1, l, blk)
                d_next = c_next - c
                flux_next = coef[0, row + 5, l, blk] * (
                    c + coef[1, row + 5, l, blk] * minmod(d, d_next)
                )
                swept.append(c - (flux_next - flux))
                after += [c_next, d_next, flux_next]
            for l in range(2):
                c0, c1 = swept[2 * l], swept[2 * l + 1]
                m0, m1 = from_left(c0, c1)
                d0, d1 = c0 - m0, c1 - m1
                e0, e1 = from_right(d0, d1)
                g0 = coef[2, row + 4, l, 0] * (c0 + coef[3, row + 4, l, 0] * minmod(d0, e0))
                g1 = coef[2, row + 4, l, 1] * (c1 + coef[3, row + 4, l, 1] * minmod(d1, e1))
                h0, h1 = from_left(g0, g1)
                swept[2 * l] = c0 - (g0 - h0)
                swept[2 * l + 1] = c1 - (g1 - h1)
            for blk in range(2):
                c0, c1 = swept[blk], swept[2 + blk]
                rise = c1 - c0
                g0 = coef[4, row + 4, 0, blk] * (c0 + coef[5, row + 4, 0, blk] * minmod(c0, rise))
                g1 = coef[4, row + 4, 1, blk] * (c1 + coef[5, row + 4, 1, blk] * minmod(rise, -c1))
                write(row, 0, blk, c0 - g0)
                write(row, 1, blk, c1 - (g1 - g0))
            return tuple(after)

        def several(n, state):
            for j in range(UNROLL):
                state = body(n * UNROLL + j, state)
            return state

        state = lax.fori_loop(0, count // UNROLL, several, tuple(state))
        for j in range(count - count % UNROLL, count):
            state = body(j, state)

    def all_copy(g, i):
        to = lax.rem(t + i, groups)
        return pltpu.make_async_remote_copy(
            src_ref=packed.at[g, to],
            dst_ref=cells_out.at[pl.ds(t * species_here + g * GROUP, GROUP)],
            send_sem=all_send.at[g, i - 1],
            recv_sem=all_recv.at[g, i - 1],
            device_id=(s, to),
            device_id_type=MESH,
        )

    def own_copy(g):
        return pltpu.make_async_copy(
            packed.at[g, t],
            cells_out.at[pl.ds(t * species_here + g * GROUP, GROUP)],
            own_sem.at[g],
        )

    packed_flat = packed.reshape(n_groups * groups * GROUP * 8, 128)
    order = [i for i in range(1, groups) if i % 2 == 1] + [i for i in range(1, groups) if i % 2 == 0]

    def halos_gone(g, carry):
        @pl.when(has_high)
        def _():
            halo_up(g).wait_send()

        return carry

    def sweep_group(g, carry):
        @pl.when(has_low)
        def _():
            halo_up(g).wait_recv()

        @pl.when(has_high)
        def _():
            halo_down(g).wait_recv()

        def put2(row, l, blk, v):
            second[row + 4, l, blk] = v

        def put3(row, l, blk, v):
            third[row + 2, l, blk] = v

        def put4(row, l, blk, v):
            start = (g * groups + row // 2) * (GROUP * 8) + l * 4 + blk * 2 + row % 2
            packed_flat[pl.ds(start, GROUP, stride=8), :] = v

        one_step(lambda row, l, blk: first[g, row + LOW, l, blk], -4, rows + 6, put2)
        one_step(lambda row, l, blk: second[row + 4, l, blk], -2, rows + 3, put3)
        one_step(lambda row, l, blk: third[row + 2, l, blk], 0, rows, put4)

        @pl.when(g == 0)
        def _():
            lax.fori_loop(0, n_groups, halos_gone, 0)

        for i in order:
            all_copy(g, i).start()
        own_copy(g).start()
        return carry

    lax.fori_loop(0, n_groups, sweep_group, 0)

    for copy in small_in:
        copy.wait()
    for l in range(2):
        for blk in range(2):
            lit_out[l * 4 + blk * 2 : l * 4 + blk * 2 + 2, :] = jnp.broadcast_to(
                mask_here[l, :, blk : blk + 1].astype(F32), (2, 128)
            )
    cold = 1.0 - sky[0]
    light = sky[1] * lit_out[...]
    reactions = rates.shape[0]
    for q in range(3):
        for j in range(reactions // 128):
            n = q * (reactions // 128) + j
            table[n : n + 1, :] = species_of[q : q + 1, j * 128 : j * 128 + 128] * 8

    ways = reactions // 128

    def rate(i, carry):
        for j in range(2):
            for w in range(ways):
                r = w * 128 + 2 * i + j
                rates[(2 * i + j) * ways + w] = (
                    coefs[r] * jnp.exp(coefs[1024 + r] * cold) + coefs[2048 + r] * light
                )
        return carry

    lax.fori_loop(0, 128 // 2, rate, 0)
    rate_copy = pltpu.make_async_copy(rates, rates_out, rate_sem.at[0])
    rate_copy.start()
    table_copy = pltpu.make_async_copy(table, table_out, rate_sem.at[1])
    table_copy.start()

    @pl.when(has_high)
    def _():
        coef_up().wait_send()

    @pl.when(has_low)
    def _():
        coef_down().wait_send()

    def finish(g, carry):
        @pl.when(has_low)
        def _():
            halo_down(g).wait_send()

        own_copy(g).wait()
        for i in order:
            all_copy(g, i).wait_send()
            source = lax.rem(t + groups - i, groups)
            pltpu.make_async_remote_copy(
                src_ref=packed.at[g, source],
                dst_ref=cells_out.at[pl.ds(source * species_here + g * GROUP, GROUP)],
                send_sem=all_send.at[g, i - 1],
                recv_sem=all_recv.at[g, i - 1],
                device_id=(s, source),
                device_id_type=MESH,
            ).wait_recv()
        return carry

    lax.fori_loop(0, n_groups, finish, 0)
    rate_copy.wait()
    table_copy.wait()


def chemistry_kernel(ways, table_in, cells_in, rates_in, lit_in, out, *scratch):
    cells, rates, lit, result, middle = scratch[:5]
    sums = scratch[5 : 5 + 6 * DAY_STEPS]
    table = scratch[5 + 6 * DAY_STEPS : 5 + 6 * DAY_STEPS + 3 * ways]
    first_sem, table_sem, rate_sem, out_sem = scratch[-4:]
    species = cells.shape[0] // 8
    zero = jnp.zeros((8, 128), F32)
    at8 = lambda i: pl.ds(pl.multiple_of(i, 8), 8)
    first_in = [
        pltpu.make_async_copy(source, target, first_sem.at[i])
        for i, (source, target) in enumerate(((cells_in, cells), (lit_in, lit)))
    ] + [
        pltpu.make_async_copy(table_in.at[pl.ds(n * 128, 128)], table[n], table_sem.at[n])
        for n in range(3 * ways)
    ]
    part = 128 // CHUNKS

    def rates_piece(i):
        where = pl.ds(pl.multiple_of(i * part * ways * 8, 8), part * ways * 8)
        return pltpu.make_async_copy(rates_in.at[where, :], rates.at[where, :], rate_sem.at[i])

    for copy in first_in:
        copy.start()
    for i in range(CHUNKS):
        rates_piece(i).start()

    def clear(i, carry):
        for j in range(4):
            for ref in sums:
                ref[at8(i * 32 + j * 8), :] = zero
        return carry

    lax.fori_loop(0, species // 4, clear, 0)
    for copy in first_in:
        copy.wait()
    day = lit[...]
    steps = (1.0 - 0.5 * day, 0.5 * day)
    piece = species // PIECES

    def out_piece(i):
        where = pl.ds(pl.multiple_of(i * piece * 8, 8), piece * 8)
        return pltpu.make_async_copy(result.at[where, :], out.at[where, :], out_sem.at[i])

    for number in range(DAY_STEPS):
        last = number == DAY_STEPS - 1
        source = cells if number == 0 else middle
        target = result if last else middle
        h = steps[number]
        made, lost_a, lost_b = (sums[6 * number + 2 * n : 6 * number + 2 * n + 2] for n in range(3))

        def react(n, carry):
            for j in range(ROUND):
                i = n * ROUND + j
                for w in range(0, ways, 2):
                    new = []
                    for k in range(2):
                        a, b, p = (at8(table[q * ways + w + k][i]) for q in range(3))
                        rate = rates[at8(n * (ROUND * ways * 8) + (j * ways + w + k) * 8), :]
                        ca, cb = source[a, :], source[b, :]
                        by_a = rate * cb
                        new.append((made[k], p, made[k][p, :] + by_a * ca))
                        new.append((lost_a[k], a, lost_a[k][a, :] + by_a))
                        new.append((lost_b[k], b, lost_b[k][b, :] + rate * ca))
                    for ref, where, value in new:
                        ref[where, :] = value
            return carry

        if number == 0:

            def react_chunk(i, carry):
                rates_piece(i).wait()
                return lax.fori_loop(i * (part // ROUND), (i + 1) * (part // ROUND), react, carry)

            lax.fori_loop(0, CHUNKS, react_chunk, 0)
        else:
            lax.fori_loop(0, 128 // ROUND, react, 0)

        def update(i, carry):
            for j in range(32):
                o = at8(i * 256 + j * 8)
                gain = made[0][o, :] + made[1][o, :]
                loss = (lost_a[0][o, :] + lost_a[1][o, :]) + (lost_b[0][o, :] + lost_b[1][o, :])
                target[o, :] = (source[o, :] + h * gain) / (1.0 + h * loss)
            return carry

        def update_piece(i, carry):
            lax.fori_loop(i * (piece // 32), (i + 1) * (piece // 32), update, 0)
            out_piece(i).start()
            return carry

        if last:
            lax.fori_loop(0, PIECES, update_piece, 0)
        else:
            lax.fori_loop(0, species // 32, update, 0)
    for i in range(PIECES):
        out_piece(i).wait()


def body(
    strips,
    groups,
    mixing_ratio_field,
    eastward_face_cfl,
    northward_face_cfl,
    upward_face_cfl,
    thermal_anomaly,
    radiant_flux,
    daylight_mask,
    baseline_kinetic_coefficient,
    arrhenius_barrier,
    photodissociation_factor,
    stoichiometry_table,
):
    species_here, levels, rows, width = mixing_ratio_field.shape
    species = species_here * groups
    reactions = baseline_kinetic_coefficient.shape[0]
    n_groups = species_here // GROUP

    def eight(x):
        return x.reshape(2, 2, 2, 128).transpose(0, 2, 1, 3).reshape(8, 128)

    vmem = pl.BlockSpec(memory_space=pltpu.VMEM)
    hbm = pl.BlockSpec(memory_space=pltpu.HBM)
    dma = pltpu.SemaphoreType.DMA
    cells, rates, table, lit = pl.pallas_call(
        functools.partial(transport_kernel, strips, groups),
        out_shape=(
            jax.ShapeDtypeStruct((species, 8, 128), F32),
            jax.ShapeDtypeStruct((reactions, 8, 128), F32),
            jax.ShapeDtypeStruct((24, 128), jnp.int32),
            jax.ShapeDtypeStruct((8, 128), F32),
        ),
        in_specs=[hbm] * 11,
        out_specs=(hbm, hbm, hbm, vmem),
        scratch_shapes=[
            pltpu.VMEM((2, species_here, 2, rows, 128), F32),
            pltpu.VMEM((n_groups, rows + LOW + HIGH, 2, 2, GROUP, 128), F32),
            pltpu.VMEM((rows + 6, 2, 2, GROUP, 128), F32),
            pltpu.VMEM((rows + 3, 2, 2, GROUP, 128), F32),
            pltpu.VMEM((n_groups, groups, GROUP, 8, 128), F32),
            pltpu.VMEM((6, rows + 7, 2, 2, GROUP, 128), F32),
            pltpu.VMEM((3, 2, 2, rows, 128), F32),
            pltpu.VMEM((3, 2, 8, 128), F32),
            pltpu.VMEM((3, 2, 8, 128), F32),
            pltpu.VMEM((3, 2, 8, 128), F32),
            pltpu.VMEM((3, 2, 8, 128), F32),
            pltpu.VMEM((reactions, 8, 128), F32),
            pltpu.VMEM((2, 8, 128), F32),
            pltpu.VMEM((2, 2, 2), jnp.int32),
            pltpu.SMEM((3 * 1024,), F32),
            pltpu.VMEM((3, reactions), jnp.int32),
            pltpu.VMEM((24, 128), jnp.int32),
            dma((n_groups, 2)),
            dma((3, 2)),
            dma((7,)),
            dma((2, n_groups)),
            dma((2, n_groups)),
            dma((2,)),
            dma((2,)),
            dma((n_groups, groups - 1)),
            dma((n_groups, groups - 1)),
            dma((n_groups,)),
            dma((2,)),
        ],
        compiler_params=pltpu.CompilerParams(
            collective_id=0, has_side_effects=True, vmem_limit_bytes=VMEM_BYTES
        ),
        name="transport",
    )(
        mixing_ratio_field,
        eastward_face_cfl,
        northward_face_cfl,
        upward_face_cfl,
        eight(thermal_anomaly),
        eight(radiant_flux),
        daylight_mask,
        baseline_kinetic_coefficient,
        arrhenius_barrier,
        photodissociation_factor,
        stoichiometry_table,
    )
    out = pl.pallas_call(
        functools.partial(chemistry_kernel, reactions // 128),
        out_shape=jax.ShapeDtypeStruct((species * 8, 128), F32),
        in_specs=[hbm] * 4,
        out_specs=hbm,
        scratch_shapes=[
            pltpu.VMEM((species * 8, 128), F32),
            pltpu.VMEM((reactions * 8, 128), F32),
            pltpu.VMEM((8, 128), F32),
        ]
        + [pltpu.VMEM((species * 8, 128), F32)] * (2 + 6 * DAY_STEPS)
        + [pltpu.SMEM((128,), jnp.int32)] * (3 * (reactions // 128))
        + [dma((2,)), dma((3 * (reactions // 128),)), dma((CHUNKS,)), dma((PIECES,))],
        compiler_params=pltpu.CompilerParams(vmem_limit_bytes=VMEM_BYTES),
        name="chemistry",
    )(
        table.reshape(24 * 128),
        cells.reshape(species * 8, 128),
        rates.reshape(reactions * 8, 128),
        lit,
    )
    return out.reshape(species, 2, 2, 2, 128).transpose(0, 1, 3, 2, 4).reshape(species, 2, 2, 256)


def solution(mesh):
    placed = (
        P("tracer", None, "space", None),
        P(None, "space", None),
        P(None, "space", None),
        P(None, "space", None),
        P(None, ("space", "tracer"), None),
        P(None, ("space", "tracer"), None),
        P(None, ("space", "tracer"), None),
        P(),
        P(),
        P(),
        P(),
    )
    return jax.shard_map(
        functools.partial(body, mesh.shape["space"], mesh.shape["tracer"]),
        mesh=mesh,
        in_specs=placed,
        out_specs=P(None, None, ("space", "tracer"), None),
        check_vma=False,
    )
```

```python
import functools

import jax
import jax.numpy as jnp
from jax import lax
from jax.experimental import pallas as pl
from jax.experimental.pallas import tpu as pltpu
from jax.sharding import PartitionSpec as P

MESH = pl.DeviceIdType.MESH
F32 = jnp.float32

SECTIONS = 3
DAY_STEPS = 2
LOW, HIGH = 2 * SECTIONS, SECTIONS
UNROLL = 8
VMEM_BYTES = 60 << 20
ROUND = 8
CHUNKS = 2
PIECES = 8
GROUP = 8


def minmod(a, b):
    return jnp.maximum(jnp.minimum(a, jnp.maximum(b, 0.0)), jnp.minimum(b, 0.0))


def transport_kernel(
    strips,
    groups,
    field,
    ux,
    uy,
    uz,
    warm,
    glow,
    mask,
    base,
    barrier_coef,
    photo,
    stoichiometry,
    cells_out,
    rates_out,
    table_out,
    lit_out,
    raw,
    first,
    second,
    third,
    packed,
    coef,
    plain,
    edge_up,
    edge_down,
    got_low,
    got_high,
    rates,
    sky,
    mask_here,
    coefs,
    species_of,
    table,
    load_sem,
    plain_sem,
    small_sem,
    halo_send,
    halo_recv,
    edge_send,
    edge_recv,
    all_send,
    all_recv,
    own_sem,
    rate_sem,
):
    s = lax.axis_index("space")
    t = lax.axis_index("tracer")
    n_groups = first.shape[0]
    rows = 16
    species_here = n_groups * GROUP
    has_low = s > 0
    has_high = s < strips - 1
    low, high = s - 1, s + 1

    def load(g, blk):
        return pltpu.make_async_copy(
            field.at[pl.ds(g * GROUP, GROUP), :, :, pl.ds(blk * 128, 128)],
            raw.at[blk, pl.ds(g * GROUP, GROUP)],
            load_sem.at[g, blk],
        )

    for g in range(n_groups):
        for blk in range(2):
            load(g, blk).start()

    plain_in = [
        pltpu.make_async_copy(
            u.at[:, :, pl.ds(blk * 128, 128)], plain.at[q, blk], plain_sem.at[q, blk]
        )
        for q, u in enumerate((ux, uy, uz))
        for blk in range(2)
    ]
    small_in = [
        pltpu.make_async_copy(source, target, small_sem.at[i])
        for i, (source, target) in enumerate(
            (
                (warm, sky.at[0]),
                (glow, sky.at[1]),
                (mask, mask_here),
                (stoichiometry, species_of),
                (base, coefs.at[pl.ds(0, base.shape[0])]),
                (barrier_coef, coefs.at[pl.ds(1024, base.shape[0])]),
                (photo, coefs.at[pl.ds(2048, base.shape[0])]),
            )
        )
    ]
    for copy in plain_in + small_in:
        copy.start()

    door = pltpu.get_barrier_semaphore()
    for i in range(1, groups):
        pl.semaphore_signal(
            door, inc=1, device_id=(s, lax.rem(t + i, groups)), device_id_type=MESH
        )

    @pl.when(has_low)
    def _():
        pl.semaphore_signal(door, inc=1, device_id=(low, t), device_id_type=MESH)

    @pl.when(has_high)
    def _():
        pl.semaphore_signal(door, inc=1, device_id=(high, t), device_id_type=MESH)

    for copy in plain_in:
        copy.wait()
    for q in range(3):
        for blk in range(2):
            for l in range(2):
                edge_up[q, blk, l * 4 : l * 4 + 4] = plain[q, blk, l, rows - 4 : rows]
                edge_down[q, blk, l * 4 : l * 4 + 4] = plain[q, blk, l, 0:4]

    block_rows = (species_here + GROUP) * 2 * rows
    flat = raw.reshape(2 * block_rows, 128)

    def turn(g, row):
        for l in range(2):
            for blk in range(2):
                start = blk * block_rows + g * (GROUP * 2 * rows) + l * rows + row
                first[g, row + LOW, l, blk] = flat[pl.ds(start, GROUP, stride=2 * rows), :]

    def halo_up(g):
        return pltpu.make_async_remote_copy(
            src_ref=first.at[g, pl.ds(rows, LOW)],
            dst_ref=first.at[g, pl.ds(0, LOW)],
            send_sem=halo_send.at[0, g],
            recv_sem=halo_recv.at[0, g],
            device_id=(high, t),
            device_id_type=MESH,
        )

    def halo_down(g):
        return pltpu.make_async_remote_copy(
            src_ref=first.at[g, pl.ds(LOW, HIGH)],
            dst_ref=first.at[g, pl.ds(LOW + rows, HIGH)],
            send_sem=halo_send.at[1, g],
            recv_sem=halo_recv.at[1, g],
            device_id=(low, t),
            device_id_type=MESH,
        )

    def coef_up():
        return pltpu.make_async_remote_copy(
            src_ref=edge_up,
            dst_ref=got_low,
            send_sem=edge_send.at[0],
            recv_sem=edge_recv.at[0],
            device_id=(high, t),
            device_id_type=MESH,
        )

    def coef_down():
        return pltpu.make_async_remote_copy(
            src_ref=edge_down,
            dst_ref=got_high,
            send_sem=edge_send.at[1],
            recv_sem=edge_recv.at[1],
            device_id=(low, t),
            device_id_type=MESH,
        )

    def turn_edges(g, carry):
        load(g, 0).wait()
        load(g, 1).wait()
        for row in (*range(HIGH), *range(rows - LOW, rows)):
            turn(g, row)
        return carry

    lax.fori_loop(0, n_groups, turn_edges, 0)

    pl.semaphore_wait(door, groups - 1 + jnp.where(has_low, 1, 0) + jnp.where(has_high, 1, 0))

    @pl.when(has_high)
    def _():
        coef_up().start()

    @pl.when(has_low)
    def _():
        coef_down().start()

    def send_up(g, carry):
        @pl.when(has_high)
        def _():
            halo_up(g).start()

        return carry

    lax.fori_loop(0, n_groups, send_up, 0)

    def send_down(g, carry):
        @pl.when(has_low)
        def _():
            halo_down(g).start()

        return carry

    lax.fori_loop(0, n_groups, send_down, 0)

    def turn_rest(g, carry):
        for row in range(HIGH, rows - LOW):
            turn(g, row)
        return carry

    lax.fori_loop(0, n_groups, turn_rest, 0)

    zero = jnp.zeros((GROUP, 128), F32)

    @pl.when(jnp.logical_not(has_low))
    def _():
        for g in range(n_groups):
            for row in range(LOW):
                for l in range(2):
                    for blk in range(2):
                        first[g, row, l, blk] = zero
        for q in range(3):
            for blk in range(2):
                got_low[q, blk] = zero

    @pl.when(jnp.logical_not(has_high))
    def _():
        for g in range(n_groups):
            for row in range(HIGH):
                for l in range(2):
                    for blk in range(2):
                        first[g, LOW + rows + row, l, blk] = zero
        for q in range(3):
            for blk in range(2):
                got_high[q, blk] = zero

    lane = lax.broadcasted_iota(jnp.int32, (GROUP, 128), 1)
    is_first = lane == 0
    is_last = lane == 127

    def from_left(x0, x1):
        r0, r1 = pltpu.roll(x0, 1, 1), pltpu.roll(x1, 1, 1)
        return jnp.where(is_first, r1, r0), jnp.where(is_first, r0, r1)

    def from_right(x0, x1):
        r0, r1 = pltpu.roll(x0, 127, 1), pltpu.roll(x1, 127, 1)
        return jnp.where(is_last, r1, r0), jnp.where(is_last, r0, r1)

    def spread(row, get):
        for l in range(2):
            for q in range(3):
                pair = [jnp.broadcast_to(get(q, l, blk), (GROUP, 128)) for blk in range(2)]
                if q == 1:
                    pair = from_right(*pair)
                for blk in range(2):
                    coef[2 * q, row, l, blk] = pair[blk]
                    coef[2 * q + 1, row, l, blk] = 0.5 * (1.0 - pair[blk])

    def spread_own(row, carry):
        spread(row + 4, lambda q, l, blk: plain[q, blk, l, pl.ds(row, 1), :])
        return carry

    lax.fori_loop(0, rows, spread_own, 0)

    @pl.when(has_low)
    def _():
        coef_up().wait_recv()

    @pl.when(has_high)
    def _():
        coef_down().wait_recv()

    for i in range(4):
        spread(i, lambda q, l, blk: got_low[q, blk, l * 4 + i : l * 4 + i + 1])
    for i in range(3):
        spread(rows + 4 + i, lambda q, l, blk: got_high[q, blk, l * 4 + i : l * 4 + i + 1])

    four = [(l, blk) for l in range(2) for blk in range(2)]

    def one_step(read, lo, count, write):
        state = []
        for l, blk in four:
            c0, c1, c2 = read(lo - 2, l, blk), read(lo - 1, l, blk), read(lo, l, blk)
            d1, d2 = c1 - c0, c2 - c1
            flux = coef[0, lo + 4, l, blk] * (c1 + coef[1, lo + 4, l, blk] * minmod(d1, d2))
            state += [c2, d2, flux]

        def body(i, state):
            row = i + lo
            after, swept = [], []
            for n, (l, blk) in enumerate(four):
                c, d, flux = state[3 * n : 3 * n + 3]
                c_next = read(row + 1, l, blk)
                d_next = c_next - c
                flux_next = coef[0, row + 5, l, blk] * (
                    c + coef[1, row + 5, l, blk] * minmod(d, d_next)
                )
                swept.append(c - (flux_next - flux))
                after += [c_next, d_next, flux_next]
            for l in range(2):
                c0, c1 = swept[2 * l], swept[2 * l + 1]
                m0, m1 = from_left(c0, c1)
                d0, d1 = c0 - m0, c1 - m1
                e0, e1 = from_right(d0, d1)
                g0 = coef[2, row + 4, l, 0] * (c0 + coef[3, row + 4, l, 0] * minmod(d0, e0))
                g1 = coef[2, row + 4, l, 1] * (c1 + coef[3, row + 4, l, 1] * minmod(d1, e1))
                h0, h1 = from_left(g0, g1)
                swept[2 * l] = c0 - (g0 - h0)
                swept[2 * l + 1] = c1 - (g1 - h1)
            for blk in range(2):
                c0, c1 = swept[blk], swept[2 + blk]
                rise = c1 - c0
                g0 = coef[4, row + 4, 0, blk] * (c0 + coef[5, row + 4, 0, blk] * minmod(c0, rise))
                g1 = coef[4, row + 4, 1, blk] * (c1 + coef[5, row + 4, 1, blk] * minmod(rise, -c1))
                write(row, 0, blk, c0 - g0)
                write(row, 1, blk, c1 - (g1 - g0))
            return tuple(after)

        def several(n, state):
            for j in range(UNROLL):
                state = body(n * UNROLL + j, state)
            return state

        state = lax.fori_loop(0, count // UNROLL, several, tuple(state))
        for j in range(count - count % UNROLL, count):
            state = body(j, state)

    def all_copy(g, i):
        to = lax.rem(t + i, groups)
        return pltpu.make_async_remote_copy(
            src_ref=packed.at[g, to],
            dst_ref=cells_out.at[pl.ds(t * species_here + g * GROUP, GROUP)],
            send_sem=all_send.at[g, i - 1],
            recv_sem=all_recv.at[g, i - 1],
            device_id=(s, to),
            device_id_type=MESH,
        )

    def own_copy(g):
        return pltpu.make_async_copy(
            packed.at[g, t],
            cells_out.at[pl.ds(t * species_here + g * GROUP, GROUP)],
            own_sem.at[g],
        )

    packed_flat = packed.reshape((n_groups + 1) * groups * GROUP * 8, 128)
    order = [i for i in range(1, groups) if i % 2 == 1] + [i for i in range(1, groups) if i % 2 == 0]

    def halos_gone(g, carry):
        @pl.when(has_high)
        def _():
            halo_up(g).wait_send()

        return carry

    def sweep_group(g, carry):
        @pl.when(has_low)
        def _():
            halo_up(g).wait_recv()

        @pl.when(has_high)
        def _():
            halo_down(g).wait_recv()

        def put2(row, l, blk, v):
            second[row + 4, l, blk] = v

        def put3(row, l, blk, v):
            third[row + 2, l, blk] = v

        def put4(row, l, blk, v):
            start = (g * groups + row // 2) * (GROUP * 8) + l * 4 + blk * 2 + row % 2
            packed_flat[pl.ds(start, GROUP, stride=8), :] = v

        one_step(lambda row, l, blk: first[g, row + LOW, l, blk], -4, rows + 6, put2)
        one_step(lambda row, l, blk: second[row + 4, l, blk], -2, rows + 3, put3)
        one_step(lambda row, l, blk: third[row + 2, l, blk], 0, rows, put4)

        @pl.when(g == 0)
        def _():
            lax.fori_loop(0, n_groups, halos_gone, 0)

        for i in order:
            all_copy(g, i).start()
        own_copy(g).start()
        return carry

    lax.fori_loop(0, n_groups, sweep_group, 0)

    for copy in small_in:
        copy.wait()
    for l in range(2):
        for blk in range(2):
            lit_out[l * 4 + blk * 2 : l * 4 + blk * 2 + 2, :] = jnp.broadcast_to(
                mask_here[l, :, blk : blk + 1].astype(F32), (2, 128)
            )
    cold = 1.0 - sky[0]
    light = sky[1] * lit_out[...]
    reactions = rates.shape[0]
    for q in range(3):
        for j in range(reactions // 128):
            n = q * (reactions // 128) + j
            table[n : n + 1, :] = species_of[q : q + 1, j * 128 : j * 128 + 128] * 8

    ways = reactions // 128

    def rate(i, carry):
        for j in range(2):
            for w in range(ways):
                r = w * 128 + 2 * i + j
                rates[(2 * i + j) * ways + w] = (
                    coefs[r] * jnp.exp(coefs[1024 + r] * cold) + coefs[2048 + r] * light
                )
        return carry

    lax.fori_loop(0, 128 // 2, rate, 0)
    rate_copy = pltpu.make_async_copy(rates, rates_out, rate_sem.at[0])
    rate_copy.start()
    table_copy = pltpu.make_async_copy(table, table_out, rate_sem.at[1])
    table_copy.start()

    @pl.when(has_high)
    def _():
        coef_up().wait_send()

    @pl.when(has_low)
    def _():
        coef_down().wait_send()

    def finish(g, carry):
        @pl.when(has_low)
        def _():
            halo_down(g).wait_send()

        own_copy(g).wait()
        for i in order:
            all_copy(g, i).wait_send()
            source = lax.rem(t + groups - i, groups)
            pltpu.make_async_remote_copy(
                src_ref=packed.at[g, source],
                dst_ref=cells_out.at[pl.ds(source * species_here + g * GROUP, GROUP)],
                send_sem=all_send.at[g, i - 1],
                recv_sem=all_recv.at[g, i - 1],
                device_id=(s, source),
                device_id_type=MESH,
            ).wait_recv()
        return carry

    lax.fori_loop(0, n_groups, finish, 0)
    rate_copy.wait()
    table_copy.wait()


def chemistry_kernel(ways, table_in, cells_in, rates_in, lit_in, out, *scratch):
    cells, rates, lit, result, middle = scratch[:5]
    sums = scratch[5 : 5 + 6 * DAY_STEPS]
    table = scratch[5 + 6 * DAY_STEPS : 5 + 6 * DAY_STEPS + 3 * ways]
    first_sem, table_sem, rate_sem, out_sem = scratch[-4:]
    species = cells.shape[0] // 8
    zero = jnp.zeros((8, 128), F32)
    at8 = lambda i: pl.ds(pl.multiple_of(i, 8), 8)
    first_in = [
        pltpu.make_async_copy(source, target, first_sem.at[i])
        for i, (source, target) in enumerate(((cells_in, cells), (lit_in, lit)))
    ] + [
        pltpu.make_async_copy(table_in.at[pl.ds(n * 128, 128)], table[n], table_sem.at[n])
        for n in range(3 * ways)
    ]
    part = 128 // CHUNKS

    def rates_piece(i):
        where = pl.ds(pl.multiple_of(i * part * ways * 8, 8), part * ways * 8)
        return pltpu.make_async_copy(rates_in.at[where, :], rates.at[where, :], rate_sem.at[i])

    for copy in first_in:
        copy.start()
    for i in range(CHUNKS):
        rates_piece(i).start()

    def clear(i, carry):
        for j in range(4):
            for ref in sums:
                ref[at8(i * 32 + j * 8), :] = zero
        return carry

    lax.fori_loop(0, species // 4, clear, 0)
    for copy in first_in:
        copy.wait()
    day = lit[...]
    steps = (1.0 - 0.5 * day, 0.5 * day)
    piece = species // PIECES

    def out_piece(i):
        where = pl.ds(pl.multiple_of(i * piece * 8, 8), piece * 8)
        return pltpu.make_async_copy(result.at[where, :], out.at[where, :], out_sem.at[i])

    for number in range(DAY_STEPS):
        last = number == DAY_STEPS - 1
        source = cells if number == 0 else middle
        target = result if last else middle
        h = steps[number]
        made, lost_a, lost_b = (sums[6 * number + 2 * n : 6 * number + 2 * n + 2] for n in range(3))

        def react(n, carry):
            for j in range(ROUND):
                i = n * ROUND + j
                for w in range(0, ways, 2):
                    new = []
                    for k in range(2):
                        a, b, p = (at8(table[q * ways + w + k][i]) for q in range(3))
                        rate = rates[at8(n * (ROUND * ways * 8) + (j * ways + w + k) * 8), :]
                        ca, cb = source[a, :], source[b, :]
                        by_a = rate * cb
                        new.append((made[k], p, made[k][p, :] + by_a * ca))
                        new.append((lost_a[k], a, lost_a[k][a, :] + by_a))
                        new.append((lost_b[k], b, lost_b[k][b, :] + rate * ca))
                    for ref, where, value in new:
                        ref[where, :] = value
            return carry

        if number == 0:

            def react_chunk(i, carry):
                rates_piece(i).wait()
                return lax.fori_loop(i * (part // ROUND), (i + 1) * (part // ROUND), react, carry)

            lax.fori_loop(0, CHUNKS, react_chunk, 0)
        else:
            lax.fori_loop(0, 128 // ROUND, react, 0)

        def update(i, carry):
            for j in range(32):
                o = at8(i * 256 + j * 8)
                gain = made[0][o, :] + made[1][o, :]
                loss = (lost_a[0][o, :] + lost_a[1][o, :]) + (lost_b[0][o, :] + lost_b[1][o, :])
                target[o, :] = (source[o, :] + h * gain) / (1.0 + h * loss)
            return carry

        def update_piece(i, carry):
            lax.fori_loop(i * (piece // 32), (i + 1) * (piece // 32), update, 0)
            out_piece(i).start()
            return carry

        if last:
            lax.fori_loop(0, PIECES, update_piece, 0)
        else:
            lax.fori_loop(0, species // 32, update, 0)
    for i in range(PIECES):
        out_piece(i).wait()


def body(
    strips,
    groups,
    mixing_ratio_field,
    eastward_face_cfl,
    northward_face_cfl,
    upward_face_cfl,
    thermal_anomaly,
    radiant_flux,
    daylight_mask,
    baseline_kinetic_coefficient,
    arrhenius_barrier,
    photodissociation_factor,
    stoichiometry_table,
):
    species_here, levels, rows, width = mixing_ratio_field.shape
    species = species_here * groups
    reactions = baseline_kinetic_coefficient.shape[0]
    n_groups = species_here // GROUP

    def eight(x):
        return x.reshape(2, 2, 2, 128).transpose(0, 2, 1, 3).reshape(8, 128)

    vmem = pl.BlockSpec(memory_space=pltpu.VMEM)
    hbm = pl.BlockSpec(memory_space=pltpu.HBM)
    dma = pltpu.SemaphoreType.DMA
    cells, rates, table, lit = pl.pallas_call(
        functools.partial(transport_kernel, strips, groups),
        out_shape=(
            jax.ShapeDtypeStruct((species, 8, 128), F32),
            jax.ShapeDtypeStruct((reactions, 8, 128), F32),
            jax.ShapeDtypeStruct((24, 128), jnp.int32),
            jax.ShapeDtypeStruct((8, 128), F32),
        ),
        in_specs=[hbm] * 11,
        out_specs=(hbm, hbm, hbm, vmem),
        scratch_shapes=[
            pltpu.VMEM((2, species_here + GROUP, 2, rows, 128), F32),
            pltpu.VMEM((n_groups, rows + LOW + HIGH, 2, 2, GROUP, 128), F32),
            pltpu.VMEM((rows + 6, 2, 2, GROUP, 128), F32),
            pltpu.VMEM((rows + 3, 2, 2, GROUP, 128), F32),
            pltpu.VMEM((n_groups + 1, groups, GROUP, 8, 128), F32),
            pltpu.VMEM((6, rows + 7, 2, 2, GROUP, 128), F32),
            pltpu.VMEM((3, 2, 2, rows, 128), F32),
            pltpu.VMEM((3, 2, 8, 128), F32),
            pltpu.VMEM((3, 2, 8, 128), F32),
            pltpu.VMEM((3, 2, 8, 128), F32),
            pltpu.VMEM((3, 2, 8, 128), F32),
            pltpu.VMEM((reactions, 8, 128), F32),
            pltpu.VMEM((2, 8, 128), F32),
            pltpu.VMEM((2, 2, 2), jnp.int32),
            pltpu.SMEM((3 * 1024,), F32),
            pltpu.VMEM((3, reactions), jnp.int32),
            pltpu.VMEM((24, 128), jnp.int32),
            dma((n_groups, 2)),
            dma((3, 2)),
            dma((7,)),
            dma((2, n_groups)),
            dma((2, n_groups)),
            dma((2,)),
            dma((2,)),
            dma((n_groups, groups - 1)),
            dma((n_groups, groups - 1)),
            dma((n_groups,)),
            dma((2,)),
        ],
        compiler_params=pltpu.CompilerParams(
            collective_id=0, has_side_effects=True, vmem_limit_bytes=VMEM_BYTES
        ),
        name="transport",
    )(
        mixing_ratio_field,
        eastward_face_cfl,
        northward_face_cfl,
        upward_face_cfl,
        eight(thermal_anomaly),
        eight(radiant_flux),
        daylight_mask,
        baseline_kinetic_coefficient,
        arrhenius_barrier,
        photodissociation_factor,
        stoichiometry_table,
    )
    out = pl.pallas_call(
        functools.partial(chemistry_kernel, reactions // 128),
        out_shape=jax.ShapeDtypeStruct((species * 8, 128), F32),
        in_specs=[hbm] * 4,
        out_specs=hbm,
        scratch_shapes=[
            pltpu.VMEM((species * 8, 128), F32),
            pltpu.VMEM((reactions * 8, 128), F32),
            pltpu.VMEM((8, 128), F32),
        ]
        + [pltpu.VMEM((species * 8, 128), F32)] * (2 + 6 * DAY_STEPS)
        + [pltpu.SMEM((128,), jnp.int32)] * (3 * (reactions // 128))
        + [dma((2,)), dma((3 * (reactions // 128),)), dma((CHUNKS,)), dma((PIECES,))],
        compiler_params=pltpu.CompilerParams(vmem_limit_bytes=VMEM_BYTES),
        name="chemistry",
    )(
        table.reshape(24 * 128),
        cells.reshape(species * 8, 128),
        rates.reshape(reactions * 8, 128),
        lit,
    )
    return out.reshape(species, 2, 2, 2, 128).transpose(0, 1, 3, 2, 4).reshape(species, 2, 2, 256)


def solution(mesh):
    placed = (
        P("tracer", None, "space", None),
        P(None, "space", None),
        P(None, "space", None),
        P(None, "space", None),
        P(None, ("space", "tracer"), None),
        P(None, ("space", "tracer"), None),
        P(None, ("space", "tracer"), None),
        P(),
        P(),
        P(),
        P(),
    )
    return jax.shard_map(
        functools.partial(body, mesh.shape["space"], mesh.shape["tracer"]),
        mesh=mesh,
        in_specs=placed,
        out_specs=P(None, None, ("space", "tracer"), None),
        check_vma=False,
    )
```

```python
import functools

import jax
import jax.numpy as jnp
from jax import lax
from jax.experimental import pallas as pl
from jax.experimental.pallas import tpu as pltpu
from jax.sharding import PartitionSpec as P

MESH = pl.DeviceIdType.MESH
F32 = jnp.float32

SECTIONS = 3
DAY_STEPS = 2
LOW, HIGH = 2 * SECTIONS, SECTIONS
UNROLL = 8
VMEM_BYTES = 60 << 20
ROUND = 8
CHUNKS = 2
PIECES = 8
GROUP = 8


def minmod(a, b):
    return jnp.maximum(jnp.minimum(a, jnp.maximum(b, 0.0)), jnp.minimum(b, 0.0))


def transport_kernel(
    strips,
    groups,
    field,
    ux,
    uy,
    uz,
    warm,
    glow,
    mask,
    base,
    barrier_coef,
    photo,
    stoichiometry,
    cells_out,
    rates_out,
    table_out,
    lit_out,
    raw,
    first,
    second,
    third,
    packed,
    coef,
    plain,
    edge_up,
    edge_down,
    got_low,
    got_high,
    rates,
    sky,
    mask_here,
    coefs,
    species_of,
    table,
    load_sem,
    plain_sem,
    small_sem,
    halo_send,
    halo_recv,
    edge_send,
    edge_recv,
    all_send,
    all_recv,
    own_sem,
    rate_sem,
):
    s = lax.axis_index("space")
    t = lax.axis_index("tracer")
    n_groups = first.shape[0]
    rows = 16
    species_here = n_groups * GROUP
    has_low = s > 0
    has_high = s < strips - 1
    low, high = s - 1, s + 1

    def load(g, blk):
        return pltpu.make_async_copy(
            field.at[pl.ds(g * GROUP, GROUP), :, :, pl.ds(blk * 128, 128)],
            raw.at[blk, pl.ds(g * GROUP, GROUP)],
            load_sem.at[g, blk],
        )

    for g in range(n_groups):
        for blk in range(2):
            load(g, blk).start()

    plain_in = [
        pltpu.make_async_copy(
            u.at[:, :, pl.ds(blk * 128, 128)], plain.at[q, blk], plain_sem.at[q, blk]
        )
        for q, u in enumerate((ux, uy, uz))
        for blk in range(2)
    ]
    small_in = [
        pltpu.make_async_copy(source, target, small_sem.at[i])
        for i, (source, target) in enumerate(
            (
                (warm, sky.at[0]),
                (glow, sky.at[1]),
                (mask, mask_here),
                (stoichiometry, species_of),
                (base, coefs.at[pl.ds(0, base.shape[0])]),
                (barrier_coef, coefs.at[pl.ds(1024, base.shape[0])]),
                (photo, coefs.at[pl.ds(2048, base.shape[0])]),
            )
        )
    ]
    for copy in plain_in + small_in:
        copy.start()

    door = pltpu.get_barrier_semaphore()
    for i in range(1, groups):
        pl.semaphore_signal(
            door, inc=1, device_id=(s, lax.rem(t + i, groups)), device_id_type=MESH
        )

    @pl.when(has_low)
    def _():
        pl.semaphore_signal(door, inc=1, device_id=(low, t), device_id_type=MESH)

    @pl.when(has_high)
    def _():
        pl.semaphore_signal(door, inc=1, device_id=(high, t), device_id_type=MESH)

    for copy in plain_in:
        copy.wait()
    for q in range(3):
        for blk in range(2):
            for l in range(2):
                edge_up[q, blk, l * 4 : l * 4 + 4] = plain[q, blk, l, rows - 4 : rows]
                edge_down[q, blk, l * 4 : l * 4 + 4] = plain[q, blk, l, 0:4]

    block_rows = (species_here + GROUP) * 2 * rows
    flat = raw.reshape(2 * block_rows, 128)

    def turn(g, row):
        for l in range(2):
            for blk in range(2):
                start = blk * block_rows + g * (GROUP * 2 * rows) + l * rows + row
                first[g, row + LOW, l, blk] = flat[pl.ds(start, GROUP, stride=2 * rows), :]

    def halo_up(g):
        return pltpu.make_async_remote_copy(
            src_ref=first.at[g, pl.ds(rows, LOW)],
            dst_ref=first.at[g, pl.ds(0, LOW)],
            send_sem=halo_send.at[0, g],
            recv_sem=halo_recv.at[0, g],
            device_id=(high, t),
            device_id_type=MESH,
        )

    def halo_down(g):
        return pltpu.make_async_remote_copy(
            src_ref=first.at[g, pl.ds(LOW, HIGH)],
            dst_ref=first.at[g, pl.ds(LOW + rows, HIGH)],
            send_sem=halo_send.at[1, g],
            recv_sem=halo_recv.at[1, g],
            device_id=(low, t),
            device_id_type=MESH,
        )

    def coef_up():
        return pltpu.make_async_remote_copy(
            src_ref=edge_up,
            dst_ref=got_low,
            send_sem=edge_send.at[0],
            recv_sem=edge_recv.at[0],
            device_id=(high, t),
            device_id_type=MESH,
        )

    def coef_down():
        return pltpu.make_async_remote_copy(
            src_ref=edge_down,
            dst_ref=got_high,
            send_sem=edge_send.at[1],
            recv_sem=edge_recv.at[1],
            device_id=(low, t),
            device_id_type=MESH,
        )

    def turn_edges(g, carry):
        load(g, 0).wait()
        load(g, 1).wait()
        for row in (*range(HIGH), *range(rows - LOW, rows)):
            turn(g, row)
        return carry

    lax.fori_loop(0, n_groups, turn_edges, 0)

    pl.semaphore_wait(door, groups - 1 + jnp.where(has_low, 1, 0) + jnp.where(has_high, 1, 0))

    @pl.when(has_high)
    def _():
        coef_up().start()

    @pl.when(has_low)
    def _():
        coef_down().start()

    def send_up(g, carry):
        @pl.when(has_high)
        def _():
            halo_up(g).start()

        return carry

    lax.fori_loop(0, n_groups, send_up, 0)

    def send_down(g, carry):
        @pl.when(has_low)
        def _():
            halo_down(g).start()

        return carry

    lax.fori_loop(0, n_groups, send_down, 0)

    def turn_rest(g, carry):
        for row in range(HIGH, rows - LOW):
            turn(g, row)
        return carry

    lax.fori_loop(0, n_groups, turn_rest, 0)

    zero = jnp.zeros((GROUP, 128), F32)

    @pl.when(jnp.logical_not(has_low))
    def _():
        for g in range(n_groups):
            for row in range(LOW):
                for l in range(2):
                    for blk in range(2):
                        first[g, row, l, blk] = zero
        for q in range(3):
            for blk in range(2):
                got_low[q, blk] = zero

    @pl.when(jnp.logical_not(has_high))
    def _():
        for g in range(n_groups):
            for row in range(HIGH):
                for l in range(2):
                    for blk in range(2):
                        first[g, LOW + rows + row, l, blk] = zero
        for q in range(3):
            for blk in range(2):
                got_high[q, blk] = zero

    lane = lax.broadcasted_iota(jnp.int32, (GROUP, 128), 1)
    is_first = lane == 0
    is_last = lane == 127

    def from_left(x0, x1):
        r0, r1 = pltpu.roll(x0, 1, 1), pltpu.roll(x1, 1, 1)
        return jnp.where(is_first, r1, r0), jnp.where(is_first, r0, r1)

    def from_right(x0, x1):
        r0, r1 = pltpu.roll(x0, 127, 1), pltpu.roll(x1, 127, 1)
        return jnp.where(is_last, r1, r0), jnp.where(is_last, r0, r1)

    def spread(row, get):
        for l in range(2):
            for q in range(3):
                pair = [jnp.broadcast_to(get(q, l, blk), (GROUP, 128)) for blk in range(2)]
                if q == 1:
                    pair = from_right(*pair)
                for blk in range(2):
                    coef[2 * q, row, l, blk] = pair[blk]
                    coef[2 * q + 1, row, l, blk] = 0.5 * (1.0 - pair[blk])

    def spread_own(row, carry):
        spread(row + 4, lambda q, l, blk: plain[q, blk, l, pl.ds(row, 1), :])
        return carry

    lax.fori_loop(0, rows, spread_own, 0)

    @pl.when(has_low)
    def _():
        coef_up().wait_recv()

    @pl.when(has_high)
    def _():
        coef_down().wait_recv()

    for i in range(4):
        spread(i, lambda q, l, blk: got_low[q, blk, l * 4 + i : l * 4 + i + 1])
    for i in range(3):
        spread(rows + 4 + i, lambda q, l, blk: got_high[q, blk, l * 4 + i : l * 4 + i + 1])

    four = [(l, blk) for l in range(2) for blk in range(2)]

    def one_step(read, lo, count, write):
        state = []
        for l, blk in four:
            c0, c1, c2 = read(lo - 2, l, blk), read(lo - 1, l, blk), read(lo, l, blk)
            d1, d2 = c1 - c0, c2 - c1
            flux = coef[0, lo + 4, l, blk] * (c1 + coef[1, lo + 4, l, blk] * minmod(d1, d2))
            state += [c2, d2, flux]

        def body(i, state):
            row = i + lo
            after, swept = [], []
            for n, (l, blk) in enumerate(four):
                c, d, flux = state[3 * n : 3 * n + 3]
                c_next = read(row + 1, l, blk)
                d_next = c_next - c
                flux_next = coef[0, row + 5, l, blk] * (
                    c + coef[1, row + 5, l, blk] * minmod(d, d_next)
                )
                swept.append(c - (flux_next - flux))
                after += [c_next, d_next, flux_next]
            for l in range(2):
                c0, c1 = swept[2 * l], swept[2 * l + 1]
                m0, m1 = from_left(c0, c1)
                d0, d1 = c0 - m0, c1 - m1
                e0, e1 = from_right(d0, d1)
                g0 = coef[2, row + 4, l, 0] * (c0 + coef[3, row + 4, l, 0] * minmod(d0, e0))
                g1 = coef[2, row + 4, l, 1] * (c1 + coef[3, row + 4, l, 1] * minmod(d1, e1))
                h0, h1 = from_left(g0, g1)
                swept[2 * l] = c0 - (g0 - h0)
                swept[2 * l + 1] = c1 - (g1 - h1)
            for blk in range(2):
                c0, c1 = swept[blk], swept[2 + blk]
                rise = c1 - c0
                g0 = coef[4, row + 4, 0, blk] * (c0 + coef[5, row + 4, 0, blk] * minmod(c0, rise))
                g1 = coef[4, row + 4, 1, blk] * (c1 + coef[5, row + 4, 1, blk] * minmod(rise, -c1))
                write(row, 0, blk, c0 - g0)
                write(row, 1, blk, c1 - (g1 - g0))
            return tuple(after)

        def several(n, state):
            for j in range(UNROLL):
                state = body(n * UNROLL + j, state)
            return state

        state = lax.fori_loop(0, count // UNROLL, several, tuple(state))
        for j in range(count - count % UNROLL, count):
            state = body(j, state)

    def all_copy(g, i):
        to = lax.rem(t + i, groups)
        return pltpu.make_async_remote_copy(
            src_ref=packed.at[g, to],
            dst_ref=cells_out.at[pl.ds(t * species_here + g * GROUP, GROUP)],
            send_sem=all_send.at[g, i - 1],
            recv_sem=all_recv.at[g, i - 1],
            device_id=(s, to),
            device_id_type=MESH,
        )

    def own_copy(g):
        return pltpu.make_async_copy(
            packed.at[g, t],
            cells_out.at[pl.ds(t * species_here + g * GROUP, GROUP)],
            own_sem.at[g],
        )

    packed_flat = packed.reshape((n_groups + 1) * groups * GROUP * 8, 128)
    order = [i for i in range(1, groups) if i % 2 == 1] + [i for i in range(1, groups) if i % 2 == 0]

    def halos_gone(g, carry):
        @pl.when(has_high)
        def _():
            halo_up(g).wait_send()

        return carry

    def sweep_group(g, carry):
        @pl.when(has_low)
        def _():
            halo_up(g).wait_recv()

        @pl.when(has_high)
        def _():
            halo_down(g).wait_recv()

        def put2(row, l, blk, v):
            second[row + 4, l, blk] = v

        def put3(row, l, blk, v):
            third[row + 2, l, blk] = v

        def put4(row, l, blk, v):
            start = (g * groups + row // 2) * (GROUP * 8) + l * 4 + blk * 2 + row % 2
            packed_flat[pl.ds(start, GROUP, stride=8), :] = v

        one_step(lambda row, l, blk: first[g, row + LOW, l, blk], -4, rows + 6, put2)
        one_step(lambda row, l, blk: second[row + 4, l, blk], -2, rows + 3, put3)
        one_step(lambda row, l, blk: third[row + 2, l, blk], 0, rows, put4)

        @pl.when(g == 0)
        def _():
            lax.fori_loop(0, n_groups, halos_gone, 0)

        for i in order:
            all_copy(g, i).start()
        own_copy(g).start()
        return carry

    lax.fori_loop(0, n_groups, sweep_group, 0)

    for copy in small_in:
        copy.wait()
    for l in range(2):
        for blk in range(2):
            lit_out[l * 4 + blk * 2 : l * 4 + blk * 2 + 2, :] = jnp.broadcast_to(
                mask_here[l, :, blk : blk + 1].astype(F32), (2, 128)
            )
    cold = 1.0 - sky[0]
    light = sky[1] * lit_out[...]
    reactions = rates.shape[0]
    for q in range(3):
        for j in range(reactions // 128):
            n = q * (reactions // 128) + j
            table[n : n + 1, :] = species_of[q : q + 1, j * 128 : j * 128 + 128] * 8

    ways = reactions // 128

    def rate(i, carry):
        for j in range(2):
            for w in range(ways):
                r = w * 128 + 2 * i + j
                rates[(2 * i + j) * ways + w] = (
                    coefs[r] * jnp.exp(coefs[1024 + r] * cold) + coefs[2048 + r] * light
                )
        return carry

    lax.fori_loop(0, 128 // 2, rate, 0)
    rate_copy = pltpu.make_async_copy(rates, rates_out, rate_sem.at[0])
    rate_copy.start()
    table_copy = pltpu.make_async_copy(table, table_out, rate_sem.at[1])
    table_copy.start()

    @pl.when(has_high)
    def _():
        coef_up().wait_send()

    @pl.when(has_low)
    def _():
        coef_down().wait_send()

    def finish(g, carry):
        @pl.when(has_low)
        def _():
            halo_down(g).wait_send()

        own_copy(g).wait()
        for i in order:
            all_copy(g, i).wait_send()
            source = lax.rem(t + groups - i, groups)
            pltpu.make_async_remote_copy(
                src_ref=packed.at[g, source],
                dst_ref=cells_out.at[pl.ds(source * species_here + g * GROUP, GROUP)],
                send_sem=all_send.at[g, i - 1],
                recv_sem=all_recv.at[g, i - 1],
                device_id=(s, source),
                device_id_type=MESH,
            ).wait_recv()
        return carry

    lax.fori_loop(0, n_groups, finish, 0)
    rate_copy.wait()
    table_copy.wait()


def chemistry_kernel(ways, table_in, cells_in, rates_in, lit_in, out, *scratch):
    cells, rates, lit, result, middle = scratch[:5]
    sums = scratch[5 : 5 + 6 * DAY_STEPS]
    table = scratch[5 + 6 * DAY_STEPS : 5 + 6 * DAY_STEPS + 3 * ways // 2]
    first_sem, table_sem, rate_sem, out_sem = scratch[-4:]
    species = cells.shape[0] // 8
    zero = jnp.zeros((8, 128), F32)
    at8 = lambda i: pl.ds(pl.multiple_of(i, 8), 8)
    first_in = [
        pltpu.make_async_copy(source, target, first_sem.at[i])
        for i, (source, target) in enumerate(((cells_in, cells), (lit_in, lit)))
    ] + [
        pltpu.make_async_copy(table_in.at[pl.ds(n * 256, 256)], table[n], table_sem.at[n])
        for n in range(3 * ways // 2)
    ]
    part = 128 // CHUNKS

    def rates_piece(i):
        where = pl.ds(pl.multiple_of(i * part * ways * 8, 8), part * ways * 8)
        return pltpu.make_async_copy(rates_in.at[where, :], rates.at[where, :], rate_sem.at[i])

    for copy in first_in:
        copy.start()
    for i in range(CHUNKS):
        rates_piece(i).start()

    def clear(i, carry):
        for j in range(4):
            for ref in sums:
                ref[at8(i * 32 + j * 8), :] = zero
        return carry

    lax.fori_loop(0, species // 4, clear, 0)
    for copy in first_in:
        copy.wait()
    day = lit[...]
    steps = (1.0 - 0.5 * day, 0.5 * day)
    piece = species // PIECES

    def out_piece(i):
        where = pl.ds(pl.multiple_of(i * piece * 8, 8), piece * 8)
        return pltpu.make_async_copy(result.at[where, :], out.at[where, :], out_sem.at[i])

    for number in range(DAY_STEPS):
        last = number == DAY_STEPS - 1
        source = cells if number == 0 else middle
        target = result if last else middle
        h = steps[number]
        made, lost_a, lost_b = (sums[6 * number + 2 * n : 6 * number + 2 * n + 2] for n in range(3))

        def react(n, carry):
            for j in range(ROUND):
                i = n * ROUND + j
                for w in range(0, ways, 2):
                    new = []
                    for k in range(2):
                        a, b, p = (at8(table[(q * ways + w) // 2][k * 128 + i]) for q in range(3))
                        rate = rates[at8(n * (ROUND * ways * 8) + (j * ways + w + k) * 8), :]
                        ca, cb = source[a, :], source[b, :]
                        by_a = rate * cb
                        new.append((made[k], p, made[k][p, :] + by_a * ca))
                        new.append((lost_a[k], a, lost_a[k][a, :] + by_a))
                        new.append((lost_b[k], b, lost_b[k][b, :] + rate * ca))
                    for ref, where, value in new:
                        ref[where, :] = value
            return carry

        if number == 0:

            def react_chunk(i, carry):
                rates_piece(i).wait()
                return lax.fori_loop(i * (part // ROUND), (i + 1) * (part // ROUND), react, carry)

            lax.fori_loop(0, CHUNKS, react_chunk, 0)
        else:
            lax.fori_loop(0, 128 // ROUND, react, 0)

        def update(i, carry):
            for j in range(32):
                o = at8(i * 256 + j * 8)
                gain = made[0][o, :] + made[1][o, :]
                loss = (lost_a[0][o, :] + lost_a[1][o, :]) + (lost_b[0][o, :] + lost_b[1][o, :])
                target[o, :] = (source[o, :] + h * gain) / (1.0 + h * loss)
            return carry

        def update_piece(i, carry):
            lax.fori_loop(i * (piece // 32), (i + 1) * (piece // 32), update, 0)
            out_piece(i).start()
            return carry

        if last:
            lax.fori_loop(0, PIECES, update_piece, 0)
        else:
            lax.fori_loop(0, species // 32, update, 0)
    for i in range(PIECES):
        out_piece(i).wait()


def body(
    strips,
    groups,
    mixing_ratio_field,
    eastward_face_cfl,
    northward_face_cfl,
    upward_face_cfl,
    thermal_anomaly,
    radiant_flux,
    daylight_mask,
    baseline_kinetic_coefficient,
    arrhenius_barrier,
    photodissociation_factor,
    stoichiometry_table,
):
    species_here, levels, rows, width = mixing_ratio_field.shape
    species = species_here * groups
    reactions = baseline_kinetic_coefficient.shape[0]
    n_groups = species_here // GROUP

    def eight(x):
        return x.reshape(2, 2, 2, 128).transpose(0, 2, 1, 3).reshape(8, 128)

    vmem = pl.BlockSpec(memory_space=pltpu.VMEM)
    hbm = pl.BlockSpec(memory_space=pltpu.HBM)
    dma = pltpu.SemaphoreType.DMA
    cells, rates, table, lit = pl.pallas_call(
        functools.partial(transport_kernel, strips, groups),
        out_shape=(
            jax.ShapeDtypeStruct((species, 8, 128), F32),
            jax.ShapeDtypeStruct((reactions, 8, 128), F32),
            jax.ShapeDtypeStruct((24, 128), jnp.int32),
            jax.ShapeDtypeStruct((8, 128), F32),
        ),
        in_specs=[hbm] * 11,
        out_specs=(hbm, hbm, hbm, vmem),
        scratch_shapes=[
            pltpu.VMEM((2, species_here + GROUP, 2, rows, 128), F32),
            pltpu.VMEM((n_groups, rows + LOW + HIGH, 2, 2, GROUP, 128), F32),
            pltpu.VMEM((rows + 6, 2, 2, GROUP, 128), F32),
            pltpu.VMEM((rows + 3, 2, 2, GROUP, 128), F32),
            pltpu.VMEM((n_groups + 1, groups, GROUP, 8, 128), F32),
            pltpu.VMEM((6, rows + 7, 2, 2, GROUP, 128), F32),
            pltpu.VMEM((3, 2, 2, rows, 128), F32),
            pltpu.VMEM((3, 2, 8, 128), F32),
            pltpu.VMEM((3, 2, 8, 128), F32),
            pltpu.VMEM((3, 2, 8, 128), F32),
            pltpu.VMEM((3, 2, 8, 128), F32),
            pltpu.VMEM((reactions, 8, 128), F32),
            pltpu.VMEM((2, 8, 128), F32),
            pltpu.VMEM((2, 2, 2), jnp.int32),
            pltpu.SMEM((3 * 1024,), F32),
            pltpu.VMEM((3, reactions), jnp.int32),
            pltpu.VMEM((24, 128), jnp.int32),
            dma((n_groups, 2)),
            dma((3, 2)),
            dma((7,)),
            dma((2, n_groups)),
            dma((2, n_groups)),
            dma((2,)),
            dma((2,)),
            dma((n_groups, groups - 1)),
            dma((n_groups, groups - 1)),
            dma((n_groups,)),
            dma((2,)),
        ],
        compiler_params=pltpu.CompilerParams(
            collective_id=0, has_side_effects=True, vmem_limit_bytes=VMEM_BYTES
        ),
        name="transport",
    )(
        mixing_ratio_field,
        eastward_face_cfl,
        northward_face_cfl,
        upward_face_cfl,
        eight(thermal_anomaly),
        eight(radiant_flux),
        daylight_mask,
        baseline_kinetic_coefficient,
        arrhenius_barrier,
        photodissociation_factor,
        stoichiometry_table,
    )
    out = pl.pallas_call(
        functools.partial(chemistry_kernel, reactions // 128),
        out_shape=jax.ShapeDtypeStruct((species * 8, 128), F32),
        in_specs=[hbm] * 4,
        out_specs=hbm,
        scratch_shapes=[
            pltpu.VMEM((species * 8, 128), F32),
            pltpu.VMEM((reactions * 8, 128), F32),
            pltpu.VMEM((8, 128), F32),
        ]
        + [pltpu.VMEM((species * 8, 128), F32)] * (2 + 6 * DAY_STEPS)
        + [pltpu.SMEM((256,), jnp.int32)] * (3 * (reactions // 256))
        + [dma((2,)), dma((3 * (reactions // 256),)), dma((CHUNKS,)), dma((PIECES,))],
        compiler_params=pltpu.CompilerParams(vmem_limit_bytes=VMEM_BYTES),
        name="chemistry",
    )(
        table.reshape(24 * 128),
        cells.reshape(species * 8, 128),
        rates.reshape(reactions * 8, 128),
        lit,
    )
    return out.reshape(species, 2, 2, 2, 128).transpose(0, 1, 3, 2, 4).reshape(species, 2, 2, 256)


def solution(mesh):
    placed = (
        P("tracer", None, "space", None),
        P(None, "space", None),
        P(None, "space", None),
        P(None, "space", None),
        P(None, ("space", "tracer"), None),
        P(None, ("space", "tracer"), None),
        P(None, ("space", "tracer"), None),
        P(),
        P(),
        P(),
        P(),
    )
    return jax.shard_map(
        functools.partial(body, mesh.shape["space"], mesh.shape["tracer"]),
        mesh=mesh,
        in_specs=placed,
        out_specs=P(None, None, ("space", "tracer"), None),
        check_vma=False,
    )
```
